128 devices in a mesh: dp: 8 (over z, x_lo), ctx: 16 (over x_hi, y, core).
Axes of the slice: x: 4 (x_hi: 2, x_lo: 2; x = x_hi * 2 + x_lo), y: 4, z: 4, core: 2. Of those that a mesh axis runs over, the one named last changes fastest.
Arguments:
- queries: bfloat16 [8, 8192, 1536], P('dp', 'ctx'), may hold values from -6 to 6
- key_rows: bfloat16 [8, 8192, 1536], P('dp', 'ctx'), may hold values from -6 to 6
- values: bfloat16 [8, 8192, 1536], P('dp', 'ctx'), may hold values from -6 to 6
- saved_out: bfloat16 [8, 8192, 1536], P('dp', 'ctx'), may hold values from -6 to 6
- log_sum: float32 [8, 12, 8192], P('dp', None, 'ctx'), may hold values from 4 to 6
- out_grad: bfloat16 [8, 8192, 3072], P('dp', 'ctx'), may hold values from -6 to 6
- out_weight: bfloat16 [1536, 3072], P(('dp', 'ctx')), may hold values from -0.15625 to 0.15625
- tile_coords: int32 [64, 3], replicated, may hold values from 0 to 15, as said below
- extents: int32 [12, 3], replicated, may hold values from 0 to 1
Outputs:
- query_grad: bfloat16 [8, 8192, 1536], P('dp', 'ctx')
- key_grad: bfloat16 [8, 8192, 1536], P('dp', 'ctx')
- value_grad: bfloat16 [8, 8192, 1536], P('dp', 'ctx')
- weight_grad: float32 [1536, 3072], P(('dp', 'ctx'))
The draws below stay inside these ranges and needn't reach their ends.
Inputs may be any that keep to these rules, and one draw needn't show every extreme that they name: `tile_coords`: row t belongs to tokens t * 128 to t * 128 + 127. Column 0 is the frame tile t // 4; columns 1 and 2 are a row below 2 and a column below 2; within each frame tile every pair of them appears once, in any order.
All inputs are finite; a program needn't handle non-finite values.
Results may differ from the reference program's by a relative error of at most 0.006.
Values may be sent and summed in bfloat16 or wider, within the bound.
A program may use at most 192 MiB of HBM per device.

```python
import math
import jax
import jax.numpy as jnp
from jax import lax

D = 3072
H = 12
HEAD = 128
HD = 1536
TILE = 128
GRID_R = 2
GRID_C = 2
TOK_DEV = 512
CLIPS = 8
TOKENS = 8192
TILES = 64


def draw_tile_coords(key, part):
    key = jax.random.fold_in(key, 11)
    spatial = GRID_R * GRID_C
    frame_tiles = TILES // spatial

    def shuffled(subkey):
        return jax.random.permutation(subkey, spatial)
    orders = jax.vmap(shuffled)(jax.random.split(key, frame_tiles))
    cells = orders.reshape(-1).astype(jnp.int32)
    frame = jnp.arange(TILES, dtype=jnp.int32) // spatial
    return jnp.stack([frame, cells // GRID_C, cells % GRID_C], axis=1)


def draw_extents(key, part):
    key = jax.random.fold_in(key, 23)
    spans = jax.random.randint(key, (H, 3), 0, 2, dtype=jnp.int32)
    first = jax.random.randint(jax.random.fold_in(key, 1), (), 0, H, dtype=jnp.int32)
    second = jax.random.randint(jax.random.fold_in(key, 2), (), 0, H, dtype=jnp.int32)
    spans = spans.at[first, 0].set(1)
    spans = spans.at[second, 2].set(0)
    return spans


def shard_levels(own_key, extent, cuts, low, high):
    factor_of = 1.0
    for dim, parts in cuts:
        steps = jax.random.uniform(jax.random.fold_in(jax.random.fold_in(own_key, 6), dim), (parts,), jnp.float32, low / len(cuts), high / len(cuts))
        factor_of = factor_of * jnp.repeat(jnp.exp(steps), extent[dim] // parts).reshape((-1,) + (1,) * (len(extent) - 1 - dim))
    return factor_of


def normal_values(rng, extent, width, reach, pieces=(), kind=jnp.bfloat16):
    result = width * jax.random.normal(rng, extent, jnp.float32)
    if pieces:
        result = result * shard_levels(rng, extent, pieces, -0.22, 0.18)
    return jnp.clip(result, -reach, reach).astype(kind)


def setup_inputs(seed: int = 0) -> dict:
    streams_of = jax.random.split(jax.random.key(seed), 10)
    return {
        "queries": normal_values(streams_of[0], (CLIPS, TOKENS, HD), 1.0, 6.0, ((0, 8), (1, 16))),
        "key_rows": normal_values(streams_of[1], (CLIPS, TOKENS, HD), 1.0, 6.0, ((0, 8), (1, 16))),
        "values": normal_values(streams_of[2], (CLIPS, TOKENS, HD), 1.0, 6.0, ((0, 8), (1, 16))),
        "saved_out": normal_values(streams_of[3], (CLIPS, TOKENS, HD), 1.0, 6.0, ((0, 8), (1, 16))),
        "log_sum": jnp.clip(4.0 + 2.0 * jax.random.uniform(streams_of[4], (CLIPS, H, TOKENS), jnp.float32) ** shard_levels(streams_of[4], (CLIPS, H, TOKENS), ((0, 8), (2, 16)), -0.2, 0.2), 4.0, 6.0),
        "out_grad": normal_values(streams_of[5], (CLIPS, TOKENS, D), 1.0, 6.0, ((0, 8), (1, 16))),
        "out_weight": normal_values(streams_of[6], (HD, D), HD ** -0.5, 0.15625, ((0, 128),)),
        "tile_coords": draw_tile_coords(jax.random.fold_in(streams_of[9], 71), 0),
        "extents": draw_extents(jax.random.fold_in(streams_of[9], 71), 0),
    }


def to_half(array):
    return lax.optimization_barrier(array.astype(jnp.bfloat16)).astype(jnp.float32)

def allowed_pairs(row_coords, col_coords, spans):
    gap = jnp.abs(row_coords[:, None, :] - col_coords[None, :, :])
    return jnp.all(gap[None] <= spans[:, None, None, :], axis=-1)

def reference(queries, key_rows, values, saved_out, log_sum, out_grad, out_weight, tile_coords, extents):
    score_scale = HEAD ** (-0.5)
    d_attn = jnp.dot(out_grad.reshape(CLIPS * TOKENS, D), out_weight.T, preferred_element_type=jnp.float32)
    d_attn = d_attn.astype(jnp.bfloat16).reshape(CLIPS, TOKENS, HD)
    attn_wide = lax.optimization_barrier(d_attn).astype(jnp.float32)
    delta = lax.optimization_barrier(jnp.sum((attn_wide * saved_out.astype(jnp.float32)).reshape(CLIPS, TOKENS, H, HEAD), axis=-1))
    delta = delta.transpose(0, 2, 1)
    coords = jnp.repeat(tile_coords, TILE, axis=0)
    far = jnp.full((TOK_DEV, 3), 1 << 20, jnp.int32)
    padded_coords = jnp.concatenate([far, coords, far], axis=0)
    frames = TOKENS // TOK_DEV

    def split_heads(rows):
        return rows.reshape(rows.shape[0], H, HEAD).transpose(1, 0, 2).astype(jnp.float32)

    def join_heads(rows):
        return rows.transpose(1, 0, 2).reshape(rows.shape[1], HD)

    def one_clip(clip):
        q_clip = lax.dynamic_index_in_dim(queries, clip, 0, keepdims=False)
        k_clip = lax.dynamic_index_in_dim(key_rows, clip, 0, keepdims=False)
        v_clip = lax.dynamic_index_in_dim(values, clip, 0, keepdims=False)
        a_clip = lax.dynamic_index_in_dim(d_attn, clip, 0, keepdims=False)
        lse_clip = lax.dynamic_index_in_dim(log_sum, clip, 0, keepdims=False)
        delta_clip = lax.dynamic_index_in_dim(delta, clip, 0, keepdims=False)
        zero_rows = jnp.zeros((TOK_DEV, HD), jnp.bfloat16)
        k_padded = jnp.concatenate([zero_rows, k_clip, zero_rows], axis=0)
        v_padded = jnp.concatenate([zero_rows, v_clip, zero_rows], axis=0)

        def one_block(block):
            begin = (block * TOK_DEV).astype(jnp.int32)
            q_rows = split_heads(lax.dynamic_slice_in_dim(q_clip, begin, TOK_DEV, 0))
            a_rows = split_heads(lax.dynamic_slice_in_dim(a_clip, begin, TOK_DEV, 0))
            k_cols = split_heads(lax.dynamic_slice_in_dim(k_padded, begin, 3 * TOK_DEV, 0))
            v_cols = split_heads(lax.dynamic_slice_in_dim(v_padded, begin, 3 * TOK_DEV, 0))
            lse_rows = lax.dynamic_slice_in_dim(lse_clip, begin, TOK_DEV, 1)
            delta_rows = lax.dynamic_slice_in_dim(delta_clip, begin, TOK_DEV, 1)
            allowed = allowed_pairs(lax.dynamic_slice_in_dim(coords, begin, TOK_DEV, 0), lax.dynamic_slice_in_dim(padded_coords, begin, 3 * TOK_DEV, 0), extents)
            scores = jnp.einsum('hid,hjd->hij', q_rows, k_cols) * score_scale
            probs = jnp.where(allowed, jnp.exp(scores - lse_rows[:, :, None]), 0.0)
            probs_half = to_half(probs)
            d_probs = jnp.einsum('hid,hjd->hij', a_rows, v_cols)
            d_scores = to_half(probs * (d_probs - delta_rows[:, :, None]))
            query_part = (score_scale * jnp.einsum('hij,hjd->hid', d_scores, k_cols)).astype(jnp.bfloat16)
            key_terms = score_scale * jnp.einsum('hij,hid->hjd', d_scores, q_rows)
            value_terms = jnp.einsum('hij,hid->hjd', probs_half, a_rows)
            return (join_heads(query_part), join_heads(key_terms), join_heads(value_terms))
        query_part, key_terms, value_terms = lax.map(one_block, jnp.arange(frames, dtype=jnp.int32))

        def combine(terms):
            own = terms[:, TOK_DEV:2 * TOK_DEV]
            zero_block = jnp.zeros((1, TOK_DEV, HD), jnp.float32)
            from_next = jnp.concatenate([terms[1:, :TOK_DEV], zero_block], axis=0)
            from_prev = jnp.concatenate([zero_block, terms[:-1, 2 * TOK_DEV:]], axis=0)
            return (own + to_half(from_next) + to_half(from_prev)).astype(jnp.bfloat16).reshape(TOKENS, HD)
        return (query_part.reshape(TOKENS, HD), combine(key_terms), combine(value_terms))
    query_grad, key_grad, value_grad = lax.map(one_clip, jnp.arange(CLIPS, dtype=jnp.int32))
    weight_grad = jnp.dot(saved_out.reshape(CLIPS * TOKENS, HD).T, out_grad.reshape(CLIPS * TOKENS, D), preferred_element_type=jnp.float32) * (1.0 / math.sqrt(CLIPS * TOKENS))
    return (query_grad, key_grad, value_grad, weight_grad)
```

```python
import functools
import math

import jax
import jax.numpy as jnp
from jax import lax
from jax.experimental import pallas as pl
from jax.experimental.pallas import tpu as pltpu
from jax.sharding import PartitionSpec as P

H = 12
HEAD = 128
TILE = 128
TOK = 512
HD = 1536
D = 3072
HALF = D // 2
ROWS = 12
PAD = 16
BLK = 8 * ROWS
CUT = 1024
PARTS = ((0, CUT), (CUT, HALF))
STEPS = (1, 3, 2)
MESH = pl.DeviceIdType.MESH
F32 = jnp.float32
BF16 = jnp.bfloat16
LOG2E = math.log2(math.e)
NT = (((1,), (1,)), ((), ()))
TN = (((0,), (0,)), ((), ()))


def place():
    dp, ctx = lax.axis_index("dp"), lax.axis_index("ctx")
    return dp // 2, (ctx // 8) * 2 + dp % 2, (ctx // 2) % 4, ctx % 2


def device(z, x, y, c):
    return (z * 2 + x % 2, (x // 2) * 8 + y * 2 + c)


def block_of(z, x):
    return z * 4 + (x % 2) * 2 + x // 2


def remote(src, dst, send, recv, target):
    return pltpu.make_async_remote_copy(
        src_ref=src, dst_ref=dst, send_sem=send, recv_sem=recv,
        device_id=target, device_id_type=MESH,
    )


def greet(z, x, y, c):
    ctx = lax.axis_index("ctx")
    dp = lax.axis_index("dp")
    barrier = pltpu.get_barrier_semaphore()

    def tell(target):
        pl.semaphore_signal(barrier, inc=1, device_id=target, device_id_type=MESH)

    for dy in range(4):
        for dc in range(2):
            if dy or dc:
                tell(device(z, x, (y + dy) % 4, (c + dc) % 2))
    for step in STEPS:
        tell(device(z, (x + step) % 4, y, c))
        tell(device((z + step) % 4, x, y, c))

    @pl.when(ctx == 7)
    def _():
        tell((dp, ctx + 1))

    @pl.when(ctx == 8)
    def _():
        tell((dp, ctx - 1))

    pl.semaphore_wait(barrier, 13 + jnp.where((ctx == 7) | (ctx == 8), 1, 0))


def halo_copies(pairs, send, recv):
    dp, ctx = lax.axis_index("dp"), lax.axis_index("ctx")
    up = jnp.minimum(ctx + 1, 15)
    down = jnp.maximum(ctx - 1, 0)
    half = len(pairs) // 2
    return [
        remote(src, dst, send.at[i], recv.at[i], (dp, up if i < half else down))
        for i, (src, dst) in enumerate(pairs)
    ]


def halo_start(copies):
    ctx = lax.axis_index("ctx")
    half = len(copies) // 2

    @pl.when(ctx < 15)
    def _():
        for copy in copies[:half]:
            copy.start()

    @pl.when(ctx > 0)
    def _():
        for copy in copies[half:]:
            copy.start()


def halo_wait(copies):
    ctx = lax.axis_index("ctx")
    half = len(copies) // 2

    @pl.when(ctx < 15)
    def _():
        for copy in copies[:half]:
            copy.wait_send()
        for copy in copies[half:]:
            copy.wait_recv()

    @pl.when(ctx > 0)
    def _():
        for copy in copies[half:]:
            copy.wait_send()
        for copy in copies[:half]:
            copy.wait_recv()


def gather_kernel(
    strip, keys, vals, so, og,
    before, after, d_attn, wgrad,
    strips, full, so_sib, og_sib,
    strip_send, strip_recv, near_send, far_send, ag_recv, sib_send, sib_recv,
    ex_send, ex_recv, halo_send, halo_recv,
):
    z, x, y, c = place()
    sib = device(z, x, y, 1 - c)
    me = block_of(z, x)
    slot = y * 2 + c
    greet(z, x, y, c)

    pending = []
    number = 0
    for dy in range(4):
        for dc in range(2):
            if dy or dc:
                copy = remote(strip, strips.at[slot], strip_send.at[number], strip_recv.at[slot],
                              device(z, x, (y + dy) % 4, (c + dc) % 2))
                copy.start()
                pending.append(copy)
                number += 1
    other = pl.ds(pl.multiple_of((1 - c) * HALF, HALF), HALF)
    exchange = [
        remote(so, so_sib, ex_send.at[0], ex_recv.at[0], sib),
        remote(og.at[:, other], og_sib, ex_send.at[1], ex_recv.at[1], sib),
    ]
    for copy in exchange:
        copy.start()
    halos = halo_copies(
        [(keys, before.at[0]), (vals, before.at[1]), (keys, after.at[0]), (vals, after.at[1])],
        halo_send, halo_recv)
    halo_start(halos)
    strips[slot] = strip[...]
    for dy in range(4):
        for dc in range(2):
            if dy or dc:
                src = ((y + dy) % 4) * 2 + (c + dc) % 2
                remote(strip, strips.at[src], strip_send.at[0], strip_recv.at[src], sib).wait_recv()
    row = lax.broadcasted_iota(jnp.int32, (BLK, 8 * PAD), 0)
    col = lax.broadcasted_iota(jnp.int32, (BLK, 8 * PAD), 1)
    pick = jnp.where(col == (row // ROWS) * PAD + row % ROWS, 1.0, 0.0).astype(BF16)
    for h in range(2):
        for o in range(0, HALF, 768):
            full[h, me, :, o:o + 768] = jnp.dot(
                pick, strips[:, :, h * HALF + o:h * HALF + o + 768].reshape(8 * PAD, 768),
                preferred_element_type=F32).astype(BF16)

    def piece(half, block, part):
        low, high = PARTS[part]
        return full.at[half, block, :, low:high]

    def along(part, first, step):
        over_x = (part == 0) == first
        return device(z, (x + step) % 4, y, c) if over_x else device((z + step) % 4, x, y, c)

    def block_at(part, first, step):
        if part == 0:
            return block_of(z, (x + step) % 4)
        return block_of((z + step) % 4, x)

    for part in range(2):
        for i, step in enumerate(STEPS):
            copy = remote(piece(c, me, part), piece(c, me, part), near_send.at[part, i],
                          ag_recv.at[part, me], along(part, True, step))
            copy.start()
            pending.append(copy)

    def onward(part, block, j):
        for i, step in enumerate(STEPS):
            copy = remote(piece(c, block, part), piece(c, block, part), far_send.at[part, j, i],
                          ag_recv.at[part, block], along(part, False, step))
            copy.start()
            pending.append(copy)

    def to_sibling(part, block):
        copy = remote(piece(c, block, part), piece(c, block, part), sib_send.at[part, block],
                      sib_recv.at[part, block], sib)
        copy.start()
        pending.append(copy)

    def arrived(part, block):
        remote(piece(c, block, part), piece(c, block, part), near_send.at[part, 0],
               ag_recv.at[part, block], sib).wait_recv()

    for part in range(2):
        onward(part, me, 0)

    for copy in exchange:
        copy.wait_recv()
    mine = pl.ds(pl.multiple_of(c * HALF, HALF), HALF)

    def wgrad_rows(i, carry):
        rows = pl.ds(pl.multiple_of(i * 256, 256), 256)
        total = lax.dot_general(so[:, rows], og[:, mine], TN, preferred_element_type=F32)
        total += lax.dot_general(so_sib[:, rows], og_sib[...], TN, preferred_element_type=F32)
        wgrad[rows, :] = total.astype(BF16)
        return carry

    for j, step in enumerate(STEPS):
        for part in range(2):
            block = block_at(part, True, step)
            arrived(part, block)
            onward(part, block, j + 1)
            to_sibling(part, block)
    lax.fori_loop(0, HD // 256, wgrad_rows, 0)

    for step in STEPS:
        for inner in (0,) + STEPS:
            block = block_of((z + step) % 4, (x + inner) % 4)
            arrived(0, block)
            to_sibling(0, block)
            block = block_of((z + inner) % 4, (x + step) % 4)
            arrived(1, block)
            to_sibling(1, block)

    for step in (0,) + STEPS:
        group = (z + step) % 4
        for inner in range(4):
            block = group * 4 + inner
            for part in range(2):
                @pl.when(block != me)
                def _():
                    remote(piece(1 - c, block, part), piece(1 - c, block, part),
                           sib_send.at[part, block], sib_recv.at[part, block], sib).wait_recv()
        feats = pl.ds(pl.multiple_of(group * 4 * BLK, 4 * BLK), 4 * BLK)

        def project(i, carry):
            rows = pl.ds(pl.multiple_of(i * 256, 256), 256)
            total = jnp.zeros((256, 4 * BLK), F32)
            for h in range(2):
                weight = full[h, pl.ds(group * 4, 4)].reshape(4 * BLK, HALF)
                total += lax.dot_general(og[rows, h * HALF:(h + 1) * HALF], weight, NT,
                                         preferred_element_type=F32)
            d_attn[rows, feats] = total.astype(BF16)
            return carry

        lax.fori_loop(0, TOK // 256, project, 0)
    halo_wait(halos)
    for copy in exchange:
        copy.wait_send()
    for copy in pending:
        copy.wait_send()


def scatter_kernel(
    wgrad, to_prev, to_next,
    out, from_next, from_prev,
    got_a, sum_a, got_b, sum_b, got_a2, got_b2, packed, last,
    first_send, first_recv, second_send, second_recv, last_send, last_recv, halo_send, halo_recv,
):
    z, x, y, c = place()
    slot = y * 2 + c
    greet(z, x, y, c)
    (a0, a1), (b0, b1) = PARTS
    pending = []
    for i, step in enumerate(STEPS):
        tz, tx = (z + step) % 4, (x + step) % 4
        for part, src, dst, target in (
            (0, wgrad.at[tz, :, :, a0:a1], got_a.at[i], device(tz, x, y, c)),
            (1, wgrad.at[:, (tx % 2) * 2 + tx // 2, :, b0:b1], got_b.at[i], device(z, tx, y, c)),
        ):
            copy = remote(src, dst, first_send.at[part, i], first_recv.at[part, i], target)
            copy.start()
            pending.append(copy)
    halos = halo_copies(
        [(to_next, from_prev), (to_prev, from_next)], halo_send, halo_recv)
    halo_start(halos)
    for i in range(3):
        pending[2 * i].wait_recv()
        pending[2 * i + 1].wait_recv()
    xs = (x % 2) * 2 + x // 2
    for j in range(4):
        total = wgrad[z, j, :, a0:a1].astype(F32)
        for i in range(3):
            total += got_a[i, j].astype(F32)
        sum_a[j] = total.astype(BF16)
        total = wgrad[j, xs, :, b0:b1].astype(F32)
        for i in range(3):
            total += got_b[i, j].astype(F32)
        sum_b[j] = total.astype(BF16)
    second = []
    for i, step in enumerate(STEPS):
        tz, tx = (z + step) % 4, (x + step) % 4
        for part, src, dst, target in (
            (0, sum_a.at[(tx % 2) * 2 + tx // 2], got_a2.at[i], device(z, tx, y, c)),
            (1, sum_b.at[tz], got_b2.at[i], device(tz, x, y, c)),
        ):
            copy = remote(src, dst, second_send.at[part, i], second_recv.at[part, i], target)
            copy.start()
            second.append(copy)
    for copy in second:
        copy.wait_recv()
    row = lax.broadcasted_iota(jnp.int32, (8 * PAD, BLK), 0)
    col = lax.broadcasted_iota(jnp.int32, (8 * PAD, BLK), 1)
    spread = jnp.where(
        (col == (row // PAD) * ROWS + row % PAD) & (row % PAD < ROWS), 1.0, 0.0).astype(BF16)
    total_a = sum_a[xs].astype(F32)
    total_b = sum_b[z].astype(F32)
    for i in range(3):
        total_a += got_a2[i].astype(F32)
        total_b += got_b2[i].astype(F32)
    packed[:, :, a0:a1] = jnp.dot(spread, total_a.astype(BF16), preferred_element_type=F32).astype(
        BF16).reshape(8, PAD, a1 - a0)
    packed[:, :, b0:b1] = jnp.dot(spread, total_b.astype(BF16), preferred_element_type=F32).astype(
        BF16).reshape(8, PAD, b1 - b0)
    number = 0
    third = []
    for dy in range(4):
        for dc in range(2):
            if dy or dc:
                ty, tc = (y + dy) % 4, (c + dc) % 2
                copy = remote(packed.at[ty * 2 + tc], last.at[slot], last_send.at[number],
                              last_recv.at[slot], device(z, x, ty, tc))
                copy.start()
                third.append(copy)
                number += 1
    last[slot] = packed[slot]
    for dy in range(4):
        for dc in range(2):
            if dy or dc:
                src = ((y + dy) % 4) * 2 + (c + dc) % 2
                remote(packed.at[src], last.at[src], last_send.at[0], last_recv.at[src],
                       device(z, x, y, 1 - c)).wait_recv()
    for h in range(2):
        total = last[h].astype(F32)
        for i in range(1, 4):
            total += last[2 * i + h].astype(F32)
        out[:, h * HALF:(h + 1) * HALF] = total * (1.0 / 256.0)
    halo_wait(halos)
    for copy in pending + second + third:
        copy.wait_send()


def attention_kernel(
    coords, extents,
    q_ref, k_ref, v_ref, kp_ref, vp_ref, kn_ref, vn_ref, a_ref, o_ref, lse_ref,
    dq_ref, dk_ref, dv_ref, prev_ref, next_ref,
    table, q_s, a_s, k_s, v_s, kt_s, row_s, dqt_s,
):
    head = pl.program_id(0)
    frame = lax.axis_index("ctx")
    scale = HEAD ** (-0.5)

    @pl.when(head == 0)
    def _():
        for k in range(3):
            base = jnp.clip(frame + k - 1, 0, 15) * 4
            for t in range(4):
                r, col = coords[base + t, 1], coords[base + t, 2]
                table[0, k, r * 2 + col] = t
                table[1, k, col * 2 + r] = t

    near_f, near_r, near_c = extents[head, 0], extents[head, 1], extents[head, 2]
    order = jnp.where(near_c == 0, 1, 0)

    def rows(k, s):
        return pl.ds(pl.multiple_of(table[order, k, s] * TILE, TILE), TILE)

    for s in range(4):
        own = rows(1, s)
        here = slice(s * TILE, (s + 1) * TILE)
        q_s[here, :] = q_ref[own, :]
        a_tile = a_ref[own, :]
        a_s[here, :] = a_tile
        prod = a_tile.astype(F32) * o_ref[own, :].astype(F32)
        row_s[0:1, here] = lse_ref[:, own] * LOG2E
        row_s[1:2, here] = jnp.sum(prod.T, axis=0, keepdims=True)
    sources = ((kp_ref, vp_ref), (k_ref, v_ref), (kn_ref, vn_ref))

    def load(k):
        for s in range(4):
            here = slice(s * TILE, (s + 1) * TILE)
            tile = sources[k][0][rows(k, s), :]
            k_s[k, here, :] = tile
            kt_s[k, :, here] = tile.T
            v_s[k, here, :] = sources[k][1][rows(k, s), :]

    def put(k, s, dk, dv):
        if k == 1:
            dk_ref[rows(k, s), :] = dk
            dv_ref[rows(k, s), :] = dv
        elif k == 0:
            prev_ref[0, rows(k, s), :] = dk.astype(BF16)
            prev_ref[1, rows(k, s), :] = dv.astype(BF16)
        else:
            next_ref[0, rows(k, s), :] = dk.astype(BF16)
            next_ref[1, rows(k, s), :] = dv.astype(BF16)

    def unit(k, begin, size):
        span = slice(begin, begin + size)
        q, a = q_s[span, :], a_s[span, :]
        lse, delta = row_s[0:1, span], row_s[1:2, span]
        step = min(size, 256)
        total = None
        for at in range(begin, begin + size, step):
            part = slice(at, at + step)
            scores = lax.dot_general(k_s[k, part, :], q, NT, preferred_element_type=F32)
            probs = jnp.exp2(scores * (scale * LOG2E) - lse)
            d_probs = lax.dot_general(v_s[k, part, :], a, NT, preferred_element_type=F32)
            d_scores = (probs * (d_probs - delta)).astype(BF16)
            dv = jnp.dot(probs.astype(BF16), a, preferred_element_type=F32)
            dk = jnp.dot(d_scores, q, preferred_element_type=F32) * scale
            dqt = jnp.dot(kt_s[k, :, part], d_scores, preferred_element_type=F32)
            total = dqt if total is None else total + dqt
            for i in range(step // TILE):
                cut = slice(i * TILE, (i + 1) * TILE)
                put(k, at // TILE + i, dk[cut], dv[cut])
        if k == 1:
            dqt_s[:, span] = total
        else:
            dqt_s[:, span] += total

    def frame_of(k):
        load(k)

        @pl.when(near_r * near_c == 1)
        def _():
            unit(k, 0, 512)

        @pl.when(near_r + near_c == 1)
        def _():
            for g in range(2):
                unit(k, g * 256, 256)

        @pl.when(near_r + near_c == 0)
        def _():
            for g in range(4):
                unit(k, g * 128, 128)

    frame_of(1)
    for k, there, ref in ((0, frame > 0, prev_ref), (2, frame < 15, next_ref)):
        use = (near_f == 1) & there

        @pl.when(use)
        def _():
            frame_of(k)

        @pl.when(jnp.logical_not(use))
        def _():
            ref[...] = jnp.zeros_like(ref)

    for s in range(4):
        dq_ref[rows(1, s), :] = (dqt_s[:, s * TILE:(s + 1) * TILE].T * scale).astype(BF16)


def any_spec():
    return pl.BlockSpec(memory_space=pl.ANY)


def vmem_spec():
    return pl.BlockSpec(memory_space=pltpu.VMEM)


def shards(
    queries, key_rows, values, saved_out, log_sum, out_grad, out_weight, tile_coords, extents
):
    q, k, v, so, og = (a[0] for a in (queries, key_rows, values, saved_out, out_grad))
    strip = jnp.pad(out_weight, ((0, PAD - ROWS), (0, 0)))
    dma = pltpu.SemaphoreType.DMA
    pair = jax.ShapeDtypeStruct((2, TOK, HD), BF16)
    before, after, d_attn, wgrad = pl.pallas_call(
        gather_kernel,
        out_shape=(pair, pair, jax.ShapeDtypeStruct((TOK, HD), BF16),
                   jax.ShapeDtypeStruct((HD, HALF), BF16)),
        in_specs=[vmem_spec(), any_spec(), any_spec(), vmem_spec(), vmem_spec()],
        out_specs=(any_spec(), any_spec(), vmem_spec(), vmem_spec()),
        scratch_shapes=[
            pltpu.VMEM((8, PAD, D), BF16),
            pltpu.VMEM((2, 16, BLK, HALF), BF16),
            pltpu.VMEM((TOK, HD), BF16),
            pltpu.VMEM((TOK, HALF), BF16),
            dma((7,)), dma((8,)), dma((2, 3)), dma((2, 4, 3)), dma((2, 16)), dma((2, 16)),
            dma((2, 16)), dma((2,)), dma((2,)), dma((4,)), dma((4,)),
        ],
        compiler_params=pltpu.CompilerParams(
            collective_id=0, has_side_effects=True, vmem_limit_bytes=48 * 2**20),
        name="gather",
    )(strip, k, v, so, og)

    def col():
        return pl.BlockSpec((TOK, HEAD), lambda h, *_: (0, h))

    def pair_col(i):
        return pl.BlockSpec((None, TOK, HEAD), lambda h, *_: (i, 0, h))

    both = pl.BlockSpec((2, TOK, HEAD), lambda h, *_: (0, 0, h))
    own32 = jax.ShapeDtypeStruct((TOK, HD), F32)
    own16 = jax.ShapeDtypeStruct((TOK, HD), BF16)
    dq, dk, dv, to_prev, to_next = pl.pallas_call(
        attention_kernel,
        out_shape=(own16, own32, own32, pair, pair),
        grid_spec=pltpu.PrefetchScalarGridSpec(
            num_scalar_prefetch=2,
            grid=(H,),
            in_specs=[col(), col(), col(), pair_col(0), pair_col(1), pair_col(0), pair_col(1),
                      col(), col(), pl.BlockSpec((None, 1, TOK), lambda h, *_: (h, 0, 0))],
            out_specs=(col(),) * 3 + (both,) * 2,
            scratch_shapes=[
                pltpu.SMEM((2, 3, 4), jnp.int32),
                pltpu.VMEM((TOK, HEAD), BF16),
                pltpu.VMEM((TOK, HEAD), BF16),
                pltpu.VMEM((3, TOK, HEAD), BF16),
                pltpu.VMEM((3, TOK, HEAD), BF16),
                pltpu.VMEM((3, HEAD, TOK), BF16),
                pltpu.VMEM((8, TOK), F32),
                pltpu.VMEM((HEAD, TOK), F32),
            ],
        ),
        compiler_params=pltpu.CompilerParams(vmem_limit_bytes=48 * 2**20),
        name="attention",
    )(tile_coords, extents, q, k, v, before, before, after, after, d_attn, so,
      log_sum[0][:, None, :])

    cut_a, cut_b = CUT, HALF - CUT
    weight_grad, from_next, from_prev = pl.pallas_call(
        scatter_kernel,
        out_shape=(jax.ShapeDtypeStruct((PAD, D), F32), pair, pair),
        in_specs=[vmem_spec(), any_spec(), any_spec()],
        out_specs=(vmem_spec(), any_spec(), any_spec()),
        scratch_shapes=[
            pltpu.VMEM((3, 4, BLK, cut_a), BF16),
            pltpu.VMEM((4, BLK, cut_a), BF16),
            pltpu.VMEM((3, 4, BLK, cut_b), BF16),
            pltpu.VMEM((4, BLK, cut_b), BF16),
            pltpu.VMEM((3, BLK, cut_a), BF16),
            pltpu.VMEM((3, BLK, cut_b), BF16),
            pltpu.VMEM((8, PAD, HALF), BF16),
            pltpu.VMEM((8, PAD, HALF), BF16),
            dma((2, 3)), dma((2, 3)), dma((2, 3)), dma((2, 3)), dma((7,)), dma((8,)),
            dma((2,)), dma((2,)),
        ],
        compiler_params=pltpu.CompilerParams(
            collective_id=1, has_side_effects=True, vmem_limit_bytes=48 * 2**20),
        name="scatter",
    )(wgrad.reshape(4, 4, BLK, HALF), to_prev, to_next)
    position = lax.axis_index("ctx")
    lower, upper = position > 0, position < 15

    def combine(own, i):
        total = own + jnp.where(upper, from_next[i].astype(F32), 0.0)
        total = total + jnp.where(lower, from_prev[i].astype(F32), 0.0)
        return total.astype(BF16)[None]

    return dq[None], combine(dk, 0), combine(dv, 1), weight_grad[:ROWS]


def solution(mesh):
    return jax.shard_map(
        shards,
        mesh=mesh,
        in_specs=(
            P("dp", "ctx", None),
            P("dp", "ctx", None),
            P("dp", "ctx", None),
            P("dp", "ctx", None),
            P("dp", None, "ctx"),
            P("dp", "ctx", None),
            P(("dp", "ctx"), None),
            P(),
            P(),
        ),
        out_specs=(
            P("dp", "ctx", None),
            P("dp", "ctx", None),
            P("dp", "ctx", None),
            P(("dp", "ctx"), None),
        ),
        check_vma=False,
    )
```

```python
import functools
import math

import jax
import jax.numpy as jnp
from jax import lax
from jax.experimental import pallas as pl
from jax.experimental.pallas import tpu as pltpu
from jax.sharding import PartitionSpec as P

H = 12
HEAD = 128
TILE = 128
TOK = 512
HD = 1536
D = 3072
HALF = D // 2
ROWS = 12
PAD = 16
BLK = 8 * ROWS
CUT = 1152
PARTS = ((0, CUT), (CUT, HALF))
SUM_CUT = 768
SUM_PARTS = ((0, SUM_CUT), (SUM_CUT, HALF))
SUB = SUM_CUT // 2
STEPS = (1, 3, 2)
MESH = pl.DeviceIdType.MESH
F32 = jnp.float32
BF16 = jnp.bfloat16
LOG2E = math.log2(math.e)
NT = (((1,), (1,)), ((), ()))
TN = (((0,), (0,)), ((), ()))


def place():
    dp, ctx = lax.axis_index("dp"), lax.axis_index("ctx")
    return dp // 2, (ctx // 8) * 2 + dp % 2, (ctx // 2) % 4, ctx % 2


def device(z, x, y, c):
    return (z * 2 + x % 2, (x // 2) * 8 + y * 2 + c)


def block_of(z, x):
    return z * 4 + (x % 2) * 2 + x // 2


def remote(src, dst, send, recv, target):
    return pltpu.make_async_remote_copy(
        src_ref=src, dst_ref=dst, send_sem=send, recv_sem=recv,
        device_id=target, device_id_type=MESH,
    )


def greet(z, x, y, c):
    barrier = pltpu.get_barrier_semaphore()

    def tell(target):
        pl.semaphore_signal(barrier, inc=1, device_id=target, device_id_type=MESH)

    for dy in range(4):
        for dc in range(2):
            if dy or dc:
                tell(device(z, x, (y + dy) % 4, (c + dc) % 2))
    for step in STEPS:
        tell(device(z, (x + step) % 4, y, c))
        tell(device((z + step) % 4, x, y, c))

    ctx, dp = lax.axis_index("ctx"), lax.axis_index("dp")

    @pl.when(ctx == 7)
    def _():
        tell((dp, ctx + 1))

    @pl.when(ctx == 8)
    def _():
        tell((dp, ctx - 1))

    pl.semaphore_wait(barrier, 13 + jnp.where((ctx == 7) | (ctx == 8), 1, 0))


def halo_copies(pairs, send, recv):
    dp, ctx = lax.axis_index("dp"), lax.axis_index("ctx")
    up = jnp.minimum(ctx + 1, 15)
    down = jnp.maximum(ctx - 1, 0)
    half = len(pairs) // 2
    return [
        remote(src, dst, send.at[i], recv.at[i], (dp, up if i < half else down))
        for i, (src, dst) in enumerate(pairs)
    ]


def halo_start(copies):
    ctx = lax.axis_index("ctx")
    half = len(copies) // 2

    @pl.when(ctx < 15)
    def _():
        for copy in copies[:half]:
            copy.start()

    @pl.when(ctx > 0)
    def _():
        for copy in copies[half:]:
            copy.start()


def halo_wait(copies):
    ctx = lax.axis_index("ctx")
    half = len(copies) // 2

    @pl.when(ctx < 15)
    def _():
        for copy in copies[:half]:
            copy.wait_send()
        for copy in copies[half:]:
            copy.wait_recv()

    @pl.when(ctx > 0)
    def _():
        for copy in copies[half:]:
            copy.wait_send()
        for copy in copies[:half]:
            copy.wait_recv()


def gather_kernel(
    strip, keys, vals, so_hbm, og_hbm,
    before, after, d_attn_out, keep_a_out, send_a_out, keep_b_out, send_b_out,
    strips, full, so, og, so_sib, og_sib, turn, d_attn, keep_a, send_a, keep_b, send_b,
    strip_send, strip_recv, near_send, far_send, pass_send, ag_recv, late_recv, sib_send, sib_recv,
    ex_send, ex_recv, halo_send, halo_recv, load_sem, store_sem,
):
    z, x, y, c = place()
    sib = device(z, x, y, 1 - c)
    me = block_of(z, x)
    slot = y * 2 + c
    loads = [pltpu.make_async_copy(so_hbm, so, load_sem.at[0]),
             pltpu.make_async_copy(og_hbm, og, load_sem.at[1])]
    for copy in loads:
        copy.start()
    strips[slot, 0:ROWS] = strip[...]
    strips[slot, ROWS:PAD] = jnp.zeros((PAD - ROWS, D), BF16)
    greet(z, x, y, c)

    pending = []
    number = 0
    for dy in range(4):
        for dc in range(2):
            if dy or dc:
                copy = remote(strips.at[slot], strips.at[slot], strip_send.at[number],
                              strip_recv.at[slot], device(z, x, (y + dy) % 4, (c + dc) % 2))
                copy.start()
                pending.append(copy)
                number += 1
    other = pl.ds(pl.multiple_of((1 - c) * HALF, HALF), HALF)
    exchange = [
        remote(so_hbm, so_sib, ex_send.at[0], ex_recv.at[0], sib),
        remote(og_hbm.at[:, other], og_sib, ex_send.at[1], ex_recv.at[1], sib),
    ]
    for copy in exchange:
        copy.start()
    for dy in range(4):
        for dc in range(2):
            if dy or dc:
                src = ((y + dy) % 4) * 2 + (c + dc) % 2
                remote(strips.at[src], strips.at[src], strip_send.at[0], strip_recv.at[src],
                       sib).wait_recv()
    row = lax.broadcasted_iota(jnp.int32, (BLK, 8 * PAD), 0)
    col = lax.broadcasted_iota(jnp.int32, (BLK, 8 * PAD), 1)
    pick = jnp.where(col == (row // ROWS) * PAD + row % ROWS, 1.0, 0.0).astype(BF16)
    for h in range(2):
        for o in range(0, HALF, 768):
            full[h, me, :, o:o + 768] = jnp.dot(
                pick, strips[:, :, h * HALF + o:h * HALF + o + 768].reshape(8 * PAD, 768),
                preferred_element_type=F32).astype(BF16)

    def piece(half, block, part):
        low, high = PARTS[part]
        return full.at[half, block, :, low:high]

    def along(part, first, step):
        over_x = (part == 0) == first
        return device(z, (x + step) % 4, y, c) if over_x else device((z + step) % 4, x, y, c)

    def block_at(part, first, step):
        if part == 0:
            return block_of(z, (x + step) % 4)
        return block_of((z + step) % 4, x)

    for part in range(2):
        for i, step in enumerate(STEPS):
            copy = remote(piece(c, me, part), piece(c, me, part), near_send.at[part, i],
                          ag_recv.at[part, me], along(part, True, step))
            copy.start()
            pending.append(copy)

    def onward(part, block, j):
        for i, step in enumerate((1, 3)):
            copy = remote(piece(c, block, part), piece(c, block, part), far_send.at[part, j, i],
                          ag_recv.at[part, block], along(part, False, step))
            copy.start()
            pending.append(copy)

    def half_piece(block, part, upper):
        low, high = PARTS[part]
        return full.at[c, block, (BLK // 2 if upper else 0):(BLK if upper else BLK // 2), low:high]

    def pass_on(part, block, j, step):
        upper = step == 1
        copy = remote(half_piece(block, part, upper), half_piece(block, part, upper),
                      pass_send.at[part, j, int(upper)],
                      (late_recv if upper else ag_recv).at[part, block],
                      along(part, False, 4 - step))
        copy.start()
        pending.append(copy)

    def arrived_late(part, block):
        for upper, sem in ((False, ag_recv), (True, late_recv)):
            remote(half_piece(block, part, upper), half_piece(block, part, upper),
                   near_send.at[part, 0], sem.at[part, block], sib).wait_recv()

    def to_sibling(part, block):
        copy = remote(piece(c, block, part), piece(c, block, part), sib_send.at[part, block],
                      sib_recv.at[part, block], sib)
        copy.start()
        pending.append(copy)

    def arrived(part, block):
        remote(piece(c, block, part), piece(c, block, part), near_send.at[part, 0],
               ag_recv.at[part, block], sib).wait_recv()

    for part in range(2):
        onward(part, me, 0)

    halos = halo_copies(
        [(keys, before.at[0]), (vals, before.at[1]), (keys, after.at[0]), (vals, after.at[1])],
        halo_send, halo_recv)
    halo_start(halos)
    for copy in exchange:
        copy.wait_recv()
    for copy in loads:
        copy.wait()
    def wgrad_group(group, j):
        rows = pl.ds(pl.multiple_of(group * 4 * BLK, 4 * BLK), 4 * BLK)
        for low, high in SUM_PARTS:
            cols = pl.ds(pl.multiple_of(c * HALF + low, 128), high - low)
            total = lax.dot_general(so[:, rows], og[:, cols], TN, preferred_element_type=F32)
            total += lax.dot_general(so_sib[:, rows], og_sib[:, low:high], TN,
                                     preferred_element_type=F32)
            total = total.astype(BF16).reshape(4, BLK, high - low)
            if low:
                turn[...] = total
            elif j == 0:
                keep_a[0] = total
            elif j == 2:
                send_a[0] = total
            else:
                first, other = (keep_a, send_a) if j == 1 else (send_a, keep_a)
                first[1, :, :, :SUB] = total[:, :, :SUB]
                other[1, :, :, SUB:] = total[:, :, SUB:]
        for k in range(4):
            tx = (x + k) % 4
            total = turn[(tx % 2) * 2 + tx // 2]
            if k == 0:
                keep_b[0, group] = total
            elif k == 2:
                send_b[0, group] = total
            else:
                first, other = (keep_b, send_b) if k == 1 else (send_b, keep_b)
                first[1, group, :, :SUB] = total[:, :SUB]
                other[1, group, :, SUB:] = total[:, SUB:]

    for j, step in enumerate(STEPS):
        for part in range(2):
            block = block_at(part, True, step)
            arrived(part, block)
            onward(part, block, j + 1)
            to_sibling(part, block)
    for j in range(4):
        wgrad_group((z + j) % 4, j)
    stores = []
    for j, (src, dst) in enumerate(((keep_a, keep_a_out), (send_a, send_a_out),
                                    (keep_b, keep_b_out), (send_b, send_b_out))):
        stores.append(pltpu.make_async_copy(src, dst, store_sem.at[j]))
        stores[-1].start()

    for step in STEPS:
        for j, inner in enumerate((0,) + STEPS):
            for part in range(2):
                if part == 0:
                    block = block_of((z + step) % 4, (x + inner) % 4)
                else:
                    block = block_of((z + inner) % 4, (x + step) % 4)
                if step == 2:
                    arrived_late(part, block)
                else:
                    arrived(part, block)
                    pass_on(part, block, j, step)
                to_sibling(part, block)

    for step in (0,) + STEPS:
        group = (z + step) % 4
        for inner in range(4):
            block = group * 4 + inner
            for part in range(2):
                @pl.when(block != me)
                def _():
                    remote(piece(1 - c, block, part), piece(1 - c, block, part),
                           sib_send.at[part, block], sib_recv.at[part, block], sib).wait_recv()
        feats = pl.ds(pl.multiple_of(group * 4 * BLK, 4 * BLK), 4 * BLK)

        def project(i, carry):
            rows = pl.ds(pl.multiple_of(i * 256, 256), 256)
            total = jnp.zeros((256, 4 * BLK), F32)
            for h in range(2):
                weight = full[h, pl.ds(group * 4, 4)].reshape(4 * BLK, HALF)
                total += lax.dot_general(og[rows, h * HALF:(h + 1) * HALF], weight, NT,
                                         preferred_element_type=F32)
            d_attn[rows, feats] = total.astype(BF16)
            return carry

        lax.fori_loop(0, TOK // 256, project, 0)
        stores.append(pltpu.make_async_copy(d_attn.at[:, feats], d_attn_out.at[:, feats],
                                            store_sem.at[4 + step]))
        stores[-1].start()
    halo_wait(halos)
    for copy in stores:
        copy.wait()
    for copy in exchange:
        copy.wait_send()
    for copy in pending:
        copy.wait_send()


def scatter_kernel(
    to_prev, to_next, keep_a_in, got_a_in, keep_b_in, got_b_in,
    out, from_next, from_prev,
    keep_a, got_a, keep_b, got_b, pass_a, pass_b, more_a, more_b,
    sum_a, sum_b, got_a2, got_b2, packed, last,
    first_send, first_recv, second_send, second_recv, last_send, last_recv,
    halo_send, halo_recv, load_sem,
):
    z, x, y, c = place()
    slot = y * 2 + c
    (low_a, high_a), (low_b, high_b) = SUM_PARTS
    loads = []
    for j, (src, dst) in enumerate(((keep_a_in, keep_a), (got_a_in, got_a),
                                    (keep_b_in, keep_b), (got_b_in, got_b))):
        loads.append(pltpu.make_async_copy(src, dst, load_sem.at[j]))
        loads[-1].start()
    greet(z, x, y, c)
    halos = halo_copies([(to_next, from_prev), (to_prev, from_next)], halo_send, halo_recv)
    for copy in loads:
        copy.wait()
    first = []
    for part, (keep, got, ready, more) in enumerate(
            ((keep_a, got_a, pass_a, more_a), (keep_b, got_b, pass_b, more_b))):
        for j in range(4):
            ready[j] = (keep[1, j].astype(F32) + got[1, j].astype(F32)).astype(BF16)
        for i, (cols, step) in enumerate(((slice(0, SUB), 1), (slice(SUB, 2 * SUB), 3))):
            target = device(z, (x + step) % 4, y, c) if part else device((z + step) % 4, x, y, c)
            copy = remote(ready.at[:, :, cols], more.at[:, :, cols], first_send.at[part, i],
                          first_recv.at[part, i], target)
            copy.start()
            first.append(copy)
    halo_start(halos)
    for copy in first:
        copy.wait_recv()
    for keep, got, more, total_ref in (
            (keep_a, got_a, more_a, sum_a), (keep_b, got_b, more_b, sum_b)):
        for j in range(4):
            total = keep[0, j].astype(F32) + got[0, j].astype(F32) + more[j].astype(F32)
            total_ref[j] = total.astype(BF16)
    xs = (x % 2) * 2 + x // 2
    second = []
    for i, step in enumerate(STEPS):
        tz, tx = (z + step) % 4, (x + step) % 4
        for part, src, dst, target in (
            (0, sum_a.at[(tx % 2) * 2 + tx // 2], got_a2.at[i], device(z, tx, y, c)),
            (1, sum_b.at[tz], got_b2.at[i], device(tz, x, y, c)),
        ):
            copy = remote(src, dst, second_send.at[part, i], second_recv.at[part, i], target)
            copy.start()
            second.append(copy)
    for copy in second:
        copy.wait_recv()
    row = lax.broadcasted_iota(jnp.int32, (8 * PAD, BLK), 0)
    col = lax.broadcasted_iota(jnp.int32, (8 * PAD, BLK), 1)
    spread = jnp.where(
        (col == (row // PAD) * ROWS + row % PAD) & (row % PAD < ROWS), 1.0, 0.0).astype(BF16)
    total_a = sum_a[xs].astype(F32)
    total_b = sum_b[z].astype(F32)
    for i in range(3):
        total_a += got_a2[i].astype(F32)
        total_b += got_b2[i].astype(F32)
    packed[:, :, low_a:high_a] = jnp.dot(spread, total_a.astype(BF16), preferred_element_type=F32).astype(
        BF16).reshape(8, PAD, high_a - low_a)
    packed[:, :, low_b:high_b] = jnp.dot(spread, total_b.astype(BF16), preferred_element_type=F32).astype(
        BF16).reshape(8, PAD, high_b - low_b)
    number = 0
    third = []
    for dy in range(4):
        for dc in range(2):
            if dy or dc:
                ty, tc = (y + dy) % 4, (c + dc) % 2
                copy = remote(packed.at[ty * 2 + tc], last.at[slot], last_send.at[number],
                              last_recv.at[slot], device(z, x, ty, tc))
                copy.start()
                third.append(copy)
                number += 1
    last[slot] = packed[slot]
    for dy in range(4):
        for dc in range(2):
            if dy or dc:
                src = ((y + dy) % 4) * 2 + (c + dc) % 2
                remote(packed.at[src], last.at[src], last_send.at[0], last_recv.at[src],
                       device(z, x, y, 1 - c)).wait_recv()
    for h in range(2):
        total = last[h].astype(F32)
        for i in range(1, 4):
            total += last[2 * i + h].astype(F32)
        out[:, h * HALF:(h + 1) * HALF] = total[:ROWS] * (1.0 / 256.0)
    halo_wait(halos)
    for copy in first + second + third:
        copy.wait_send()


def attention_kernel(
    coords, extents,
    q_ref, k_ref, v_ref, kp_ref, vp_ref, kn_ref, vn_ref, a_ref, o_ref, lse_ref,
    dq_ref, dk_ref, dv_ref, prev_ref, next_ref,
    table, q_s, a_s, k_s, v_s, kt_s, row_s, dqt_s,
):
    head = pl.program_id(0)
    frame = lax.axis_index("ctx")
    scale = HEAD ** (-0.5)

    @pl.when(head == 0)
    def _():
        for k in range(3):
            base = jnp.clip(frame + k - 1, 0, 15) * 4
            for t in range(4):
                r, col = coords[base + t, 1], coords[base + t, 2]
                table[0, k, r * 2 + col] = t
                table[1, k, col * 2 + r] = t

    near_f, near_r, near_c = extents[head, 0], extents[head, 1], extents[head, 2]
    order = jnp.where(near_c == 0, 1, 0)

    def rows(k, s):
        return pl.ds(pl.multiple_of(table[order, k, s] * TILE, TILE), TILE)

    for s in range(4):
        own = rows(1, s)
        here = slice(s * TILE, (s + 1) * TILE)
        q_s[here, :] = q_ref[own, :]
        a_tile = a_ref[own, :]
        a_s[here, :] = a_tile
        prod = a_tile.astype(F32) * o_ref[own, :].astype(F32)
        row_s[0:1, here] = lse_ref[:, own] * LOG2E
        row_s[1:2, here] = jnp.sum(prod.T, axis=0, keepdims=True)
    sources = ((kp_ref, vp_ref), (k_ref, v_ref), (kn_ref, vn_ref))

    def load(k):
        for s in range(4):
            here = slice(s * TILE, (s + 1) * TILE)
            tile = sources[k][0][rows(k, s), :]
            k_s[k, here, :] = tile
            kt_s[k, :, here] = tile.T
            v_s[k, here, :] = sources[k][1][rows(k, s), :]

    def put(k, s, dk, dv):
        if k == 1:
            dk_ref[rows(k, s), :] = dk
            dv_ref[rows(k, s), :] = dv
        elif k == 0:
            prev_ref[0, rows(k, s), :] = dk.astype(BF16)
            prev_ref[1, rows(k, s), :] = dv.astype(BF16)
        else:
            next_ref[0, rows(k, s), :] = dk.astype(BF16)
            next_ref[1, rows(k, s), :] = dv.astype(BF16)

    def unit(k, begin, size):
        span = slice(begin, begin + size)
        q, a = q_s[span, :], a_s[span, :]
        lse, delta = row_s[0:1, span], row_s[1:2, span]
        step = min(size, 256)
        total = None
        for at in range(begin, begin + size, step):
            part = slice(at, at + step)
            scores = lax.dot_general(k_s[k, part, :], q, NT, preferred_element_type=F32)
            probs = jnp.exp2(scores * (scale * LOG2E) - lse)
            d_probs = lax.dot_general(v_s[k, part, :], a, NT, preferred_element_type=F32)
            d_scores = (probs * (d_probs - delta)).astype(BF16)
            dv = jnp.dot(probs.astype(BF16), a, preferred_element_type=F32)
            dk = jnp.dot(d_scores, q, preferred_element_type=F32) * scale
            dqt = jnp.dot(kt_s[k, :, part], d_scores, preferred_element_type=F32)
            total = dqt if total is None else total + dqt
            for i in range(step // TILE):
                cut = slice(i * TILE, (i + 1) * TILE)
                put(k, at // TILE + i, dk[cut], dv[cut])
        if k == 1:
            dqt_s[:, span] = total
        else:
            dqt_s[:, span] += total

    def frame_of(k):
        load(k)

        @pl.when(near_r * near_c == 1)
        def _():
            unit(k, 0, 512)

        @pl.when(near_r + near_c == 1)
        def _():
            for g in range(2):
                unit(k, g * 256, 256)

        @pl.when(near_r + near_c == 0)
        def _():
            for g in range(4):
                unit(k, g * 128, 128)

    frame_of(1)
    for k, there, ref in ((0, frame > 0, prev_ref), (2, frame < 15, next_ref)):
        use = (near_f == 1) & there

        @pl.when(use)
        def _():
            frame_of(k)

        @pl.when(jnp.logical_not(use))
        def _():
            ref[...] = jnp.zeros_like(ref)

    for s in range(4):
        dq_ref[rows(1, s), :] = (dqt_s[:, s * TILE:(s + 1) * TILE].T * scale).astype(BF16)


def combine_kernel(dk, dv, ahead, behind, key_out, value_out):
    frame = lax.axis_index("ctx")
    for i, (own, out) in enumerate(((dk, key_out), (dv, value_out))):
        total = own[...] + jnp.where(frame < 15, ahead[i].astype(F32), 0.0)
        total += jnp.where(frame > 0, behind[i].astype(F32), 0.0)
        out[...] = total.astype(BF16)


def any_spec():
    return pl.BlockSpec(memory_space=pl.ANY)


def vmem_spec():
    return pl.BlockSpec(memory_space=pltpu.VMEM)


def along_x(value, step):
    pairs = []
    for dp in range(8):
        for ctx in range(16):
            x = (ctx // 8) * 2 + dp % 2
            tx = (x + step) % 4
            pairs.append((dp * 16 + ctx, ((dp // 2) * 2 + tx % 2) * 16 + (tx // 2) * 8 + ctx % 8))
    return lax.ppermute(value, ("dp", "ctx"), pairs)


def along_z(value, step):
    return lax.ppermute(value, "dp", [(i, (i + 2 * step) % 8) for i in range(8)])


def shards(
    queries, key_rows, values, saved_out, log_sum, out_grad, out_weight, tile_coords, extents
):
    q, k, v, so, og = (a[0] for a in (queries, key_rows, values, saved_out, out_grad))
    col = pl.BlockSpec((TOK, HEAD), lambda h, *_: (0, h))
    pair = jax.ShapeDtypeStruct((2, TOK, HD), BF16)
    dma = pltpu.SemaphoreType.DMA
    moving = jax.ShapeDtypeStruct((2, 4, BLK, SUM_CUT), BF16)
    before, after, d_attn, keep_a, send_a, keep_b, send_b = pl.pallas_call(
        gather_kernel,
        out_shape=(pair, pair, jax.ShapeDtypeStruct((TOK, HD), BF16)) + (moving,) * 4,
        in_specs=[vmem_spec()] + [any_spec()] * 4,
        out_specs=(any_spec(),) * 7,
        scratch_shapes=[
            pltpu.VMEM((8, PAD, D), BF16),
            pltpu.VMEM((2, 16, BLK, HALF), BF16),
            pltpu.VMEM((TOK, HD), BF16),
            pltpu.VMEM((TOK, D), BF16),
            pltpu.VMEM((TOK, HD), BF16),
            pltpu.VMEM((TOK, HALF), BF16),
            pltpu.VMEM((4, BLK, SUM_CUT), BF16),
            pltpu.VMEM((TOK, HD), BF16),
        ] + [pltpu.VMEM((2, 4, BLK, SUM_CUT), BF16)] * 4 + [
            dma((7,)), dma((8,)), dma((2, 3)), dma((2, 4, 2)), dma((2, 4, 2)), dma((2, 16)),
            dma((2, 16)), dma((2, 16)), dma((2, 16)), dma((2,)), dma((2,)), dma((4,)), dma((4,)),
            dma((2,)), dma((8,)),
        ],
        compiler_params=pltpu.CompilerParams(
            collective_id=0, has_side_effects=True, vmem_limit_bytes=56 * 2**20),
        cost_estimate=pl.CostEstimate(
            flops=10**10, bytes_accessed=20 * 10**6, transcendentals=0),
        name="gather",
    )(out_weight, k, v, so, og)
    got_a, got_b = along_z(send_a, 2), along_x(send_b, 2)

    own32 = jax.ShapeDtypeStruct((TOK, HD), F32)
    own16 = jax.ShapeDtypeStruct((TOK, HD), BF16)
    row = pl.BlockSpec((None, 1, TOK), lambda h, *_: (h, 0, 0))

    def side(i):
        return pl.BlockSpec((None, TOK, HEAD), lambda h, *_, i=i: (i, 0, h))

    sides = pl.BlockSpec((2, TOK, HEAD), lambda h, *_: (0, 0, h))
    dq, dk, dv, to_prev, to_next = pl.pallas_call(
        attention_kernel,
        out_shape=(own16, own32, own32, pair, pair),
        grid_spec=pltpu.PrefetchScalarGridSpec(
            num_scalar_prefetch=2,
            grid=(H,),
            in_specs=[col] * 3 + [side(0), side(1)] * 2 + [col] * 2 + [row],
            out_specs=(col,) * 3 + (sides,) * 2,
            scratch_shapes=[
                pltpu.SMEM((2, 3, 4), jnp.int32),
                pltpu.VMEM((TOK, HEAD), BF16),
                pltpu.VMEM((TOK, HEAD), BF16),
                pltpu.VMEM((3, TOK, HEAD), BF16),
                pltpu.VMEM((3, TOK, HEAD), BF16),
                pltpu.VMEM((3, HEAD, TOK), BF16),
                pltpu.VMEM((8, TOK), F32),
                pltpu.VMEM((HEAD, TOK), F32),
            ],
        ),
        compiler_params=pltpu.CompilerParams(vmem_limit_bytes=48 * 2**20),
        cost_estimate=pl.CostEstimate(
            flops=12 * 10**9, bytes_accessed=30 * 10**6, transcendentals=10**7),
        name="attention",
    )(tile_coords, extents, q, k, v, before, before, after, after, d_attn, so,
      log_sum[0][:, None, :])

    weight_grad, from_next, from_prev = pl.pallas_call(
        scatter_kernel,
        out_shape=(jax.ShapeDtypeStruct((ROWS, D), F32), pair, pair),
        in_specs=[any_spec()] * 6,
        out_specs=(vmem_spec(), any_spec(), any_spec()),
        scratch_shapes=[pltpu.VMEM((2, 4, BLK, SUM_CUT), BF16)] * 4
        + [pltpu.VMEM((4, BLK, SUM_CUT), BF16)] * 6
        + [pltpu.VMEM((3, BLK, SUM_CUT), BF16)] * 2 + [
            pltpu.VMEM((8, PAD, HALF), BF16),
            pltpu.VMEM((8, PAD, HALF), BF16),
            dma((2, 2)), dma((2, 2)), dma((2, 3)), dma((2, 3)), dma((7,)), dma((8,)),
            dma((2,)), dma((2,)), dma((4,)),
        ],
        compiler_params=pltpu.CompilerParams(
            collective_id=1, has_side_effects=True, vmem_limit_bytes=48 * 2**20),
        cost_estimate=pl.CostEstimate(
            flops=10**10, bytes_accessed=20 * 10**6, transcendentals=0),
        name="scatter",
    )(to_prev, to_next, keep_a, got_a, keep_b, got_b)

    wide = HD // 4
    whole = pl.BlockSpec((TOK, wide), lambda i: (0, i))
    halo = pl.BlockSpec((2, TOK, wide), lambda i: (0, 0, i))
    key_grad, value_grad = pl.pallas_call(
        combine_kernel,
        out_shape=(own16, own16),
        grid=(4,),
        in_specs=[whole, whole, halo, halo],
        out_specs=(whole, whole),
        compiler_params=pltpu.CompilerParams(vmem_limit_bytes=48 * 2**20),
        name="combine",
    )(dk, dv, from_next, from_prev)
    return dq[None], key_grad[None], value_grad[None], weight_grad


def solution(mesh):
    return jax.shard_map(
        shards,
        mesh=mesh,
        in_specs=(
            P("dp", "ctx", None),
            P("dp", "ctx", None),
            P("dp", "ctx", None),
            P("dp", "ctx", None),
            P("dp", None, "ctx"),
            P("dp", "ctx", None),
            P(("dp", "ctx"), None),
            P(),
            P(),
        ),
        out_specs=(
            P("dp", "ctx", None),
            P("dp", "ctx", None),
            P("dp", "ctx", None),
            P(("dp", "ctx"), None),
        ),
        check_vma=False,
    )
```

```python
import functools
import functools
import math

import jax
import jax.numpy as jnp
from jax import lax
from jax.experimental import pallas as pl
from jax.experimental.pallas import tpu as pltpu
from jax.sharding import PartitionSpec as P

H = 12
HEAD = 128
TILE = 128
TOK = 512
HD = 1536
D = 3072
HALF = D // 2
ROWS = 12
PAD = 16
BLK = 8 * ROWS
CUT = 1024
PARTS = ((0, CUT), (CUT, HALF))
SUM_CUT = 768
SUM_PARTS = ((0, SUM_CUT), (SUM_CUT, HALF))
SUB = SUM_CUT // 2
STEPS = (1, 3, 2)
GROUP = 2
VMEM_LIMIT = 60 * 2**20
MESH = pl.DeviceIdType.MESH
F32 = jnp.float32
BF16 = jnp.bfloat16
LOG2E = math.log2(math.e)
NT = (((1,), (1,)), ((), ()))
TN = (((0,), (0,)), ((), ()))


def place():
    dp, ctx = lax.axis_index("dp"), lax.axis_index("ctx")
    return dp // 2, (ctx // 8) * 2 + dp % 2, (ctx // 2) % 4, ctx % 2


def device(z, x, y, c):
    return (z * 2 + x % 2, (x // 2) * 8 + y * 2 + c)


def block_of(z, x):
    return z * 4 + (x % 2) * 2 + x // 2


def remote(src, dst, send, recv, target):
    return pltpu.make_async_remote_copy(
        src_ref=src, dst_ref=dst, send_sem=send, recv_sem=recv,
        device_id=target, device_id_type=MESH,
    )


def greet(z, x, y, c):
    barrier = pltpu.get_barrier_semaphore()

    def tell(target):
        pl.semaphore_signal(barrier, inc=1, device_id=target, device_id_type=MESH)

    for dy in range(4):
        for dc in range(2):
            if dy or dc:
                tell(device(z, x, (y + dy) % 4, (c + dc) % 2))
    for step in STEPS:
        tell(device(z, (x + step) % 4, y, c))
        tell(device((z + step) % 4, x, y, c))

    ctx, dp = lax.axis_index("ctx"), lax.axis_index("dp")

    @pl.when(ctx == 7)
    def _():
        tell((dp, ctx + 1))

    @pl.when(ctx == 8)
    def _():
        tell((dp, ctx - 1))

    pl.semaphore_wait(barrier, 13 + jnp.where((ctx == 7) | (ctx == 8), 1, 0))


HALO_SEMS = [pltpu.SemaphoreType.DMA(shape) for shape in ((2,), (2,), (2, 4), (2, 4), (2, 4))]


class Halo:
    def __init__(self, ups, downs, before, after, send, recv, piece_send, piece_recv, relay_send):
        self.dp, self.ctx = lax.axis_index("dp"), lax.axis_index("ctx")
        ctx = self.ctx
        ways = (
            (ups, before, jnp.minimum(ctx + 1, 15), jnp.where(ctx == 7, 0, jnp.minimum(ctx + 1, 15)), 8),
            (downs, after, jnp.maximum(ctx - 1, 0), jnp.where(ctx == 8, 15, jnp.maximum(ctx - 1, 0)), 7),
        )
        self.straight, self.pieces, self.relays = [], [], []
        for i, (src, dst, near, first, last) in enumerate(ways):
            self.straight.append(
                remote(src[0], dst.at[0], send.at[i], recv.at[i], (self.dp, near)))
            spans = [pl.ds(j * TILE, TILE) for j in range(TOK // TILE)]
            self.pieces.append([
                remote(src[1].at[span], dst.at[1, span], piece_send.at[i, j], piece_recv.at[i, j],
                       (self.dp, first)) for j, span in enumerate(spans)])
            self.relays.append([
                remote(dst.at[1, span], dst.at[1, span], relay_send.at[i, j], piece_recv.at[i, j],
                       (self.dp, last)) for j, span in enumerate(spans)])
        self.sends = (ctx < 15, ctx > 0)
        self.gets = (ctx > 0, ctx < 15)
        self.passes = (ctx == 0, ctx == 15)

    def start(self):
        for i in range(2):
            @pl.when(self.sends[i])
            def _():
                for copy in self.pieces[i]:
                    copy.start()
                self.straight[i].start()

    def relay(self, *numbers):
        for i in range(2):
            @pl.when(self.passes[i])
            def _():
                for j in numbers:
                    self.pieces[i][j].wait_recv()
                    self.relays[i][j].start()

    def wait(self):
        for i in range(2):
            @pl.when(self.gets[i])
            def _():
                self.straight[i].wait_recv()
                for copy in self.pieces[i]:
                    copy.wait_recv()

            @pl.when(self.sends[i])
            def _():
                self.straight[i].wait_send()
                for copy in self.pieces[i]:
                    copy.wait_send()

            @pl.when(self.passes[i])
            def _():
                for onward in self.relays[i]:
                    onward.wait_send()


def gather_kernel(
    strip, keys, vals, so_hbm, og_hbm,
    before, after, d_attn_out, keep_a_out, send_a_out, keep_b_out, send_b_out,
    padded, strips, full, so, og, so_sib, og_sib, turn, d_attn, keep_a, send_a, keep_b, send_b,
    strip_send, strip_recv, near_send, far_send, pass_send, ag_recv, late_recv, sib_send, sib_recv,
    ex_send, ex_recv, load_sem, store_sem, *halo_sems,
):
    z, x, y, c = place()
    sib = device(z, x, y, 1 - c)
    me = block_of(z, x)
    slot = y * 2 + c
    loads = [pltpu.make_async_copy(so_hbm, so, load_sem.at[0]),
             pltpu.make_async_copy(og_hbm, og, load_sem.at[1])]
    for copy in loads:
        copy.start()
    for h in range(2):
        padded[h, 0:ROWS] = strip[:, h * HALF:(h + 1) * HALF]
        padded[h, ROWS:PAD] = jnp.zeros((PAD - ROWS, HALF), BF16)
    strips[slot] = padded[c]
    greet(z, x, y, c)

    pending = []
    number = 0
    for dy in range(4):
        for dc in range(2):
            if dy or dc:
                tc = (c + dc) % 2
                copy = remote(padded.at[tc], strips.at[slot], strip_send.at[number],
                              strip_recv.at[slot], device(z, x, (y + dy) % 4, tc))
                copy.start()
                pending.append(copy)
                number += 1
    other = pl.ds(pl.multiple_of((1 - c) * HALF, HALF), HALF)
    exchange = [
        remote(so_hbm, so_sib, ex_send.at[0], ex_recv.at[0], sib),
        remote(og_hbm.at[:, other], og_sib, ex_send.at[1], ex_recv.at[1], sib),
    ]
    for copy in exchange:
        copy.start()
    for dy in range(4):
        for dc in range(2):
            if dy or dc:
                src = ((y + dy) % 4) * 2 + (c + dc) % 2
                remote(strips.at[src], strips.at[src], strip_send.at[0], strip_recv.at[src],
                       sib).wait_recv()
    row = lax.broadcasted_iota(jnp.int32, (BLK, 8 * PAD), 0)
    col = lax.broadcasted_iota(jnp.int32, (BLK, 8 * PAD), 1)
    pick = jnp.where(col == (row // ROWS) * PAD + row % ROWS, 1.0, 0.0).astype(BF16)
    for o in range(0, HALF, 768):
        full[c, me, :, o:o + 768] = jnp.dot(
            pick, strips[:, :, o:o + 768].reshape(8 * PAD, 768),
            preferred_element_type=F32).astype(BF16)

    def piece(half, block, part):
        low, high = PARTS[part]
        return full.at[half, block, :, low:high]

    def along(part, first, step):
        over_x = (part == 0) == first
        return device(z, (x + step) % 4, y, c) if over_x else device((z + step) % 4, x, y, c)

    def block_at(part, first, step):
        if part == 0:
            return block_of(z, (x + step) % 4)
        return block_of((z + step) % 4, x)

    for part in range(2):
        for i, step in enumerate(STEPS):
            copy = remote(piece(c, me, part), piece(c, me, part), near_send.at[part, i],
                          ag_recv.at[part, me], along(part, True, step))
            copy.start()
            pending.append(copy)

    def onward(part, block, j):
        for i, step in enumerate((1, 3)):
            copy = remote(piece(c, block, part), piece(c, block, part), far_send.at[part, j, i],
                          ag_recv.at[part, block], along(part, False, step))
            copy.start()
            pending.append(copy)

    def half_piece(block, part, upper):
        low, high = PARTS[part]
        return full.at[c, block, (BLK // 2 if upper else 0):(BLK if upper else BLK // 2), low:high]

    def pass_on(part, block, j, step):
        upper = step == 1
        copy = remote(half_piece(block, part, upper), half_piece(block, part, upper),
                      pass_send.at[part, j, int(upper)],
                      (late_recv if upper else ag_recv).at[part, block],
                      along(part, False, 4 - step))
        copy.start()
        pending.append(copy)

    def arrived_late(part, block):
        for upper, sem in ((False, ag_recv), (True, late_recv)):
            remote(half_piece(block, part, upper), half_piece(block, part, upper),
                   near_send.at[part, 0], sem.at[part, block], sib).wait_recv()

    def to_sibling(part, block):
        copy = remote(piece(c, block, part), piece(c, block, part), sib_send.at[part, block],
                      sib_recv.at[part, block], sib)
        copy.start()
        pending.append(copy)

    def arrived(part, block):
        remote(piece(c, block, part), piece(c, block, part), near_send.at[part, 0],
               ag_recv.at[part, block], sib).wait_recv()

    for part in range(2):
        onward(part, me, 0)
        to_sibling(part, me)

    halo = Halo((keys, vals), (keys, vals), before, after, *halo_sems)
    halo.start()
    for copy in exchange:
        copy.wait_recv()
    for copy in loads:
        copy.wait()
    def wgrad_group(group, j):
        rows = pl.ds(pl.multiple_of(group * 4 * BLK, 4 * BLK), 4 * BLK)
        for low, high in SUM_PARTS:
            cols = pl.ds(pl.multiple_of(c * HALF + low, 128), high - low)
            total = lax.dot_general(so[:, rows], og[:, cols], TN, preferred_element_type=F32)
            total += lax.dot_general(so_sib[:, rows], og_sib[:, low:high], TN,
                                     preferred_element_type=F32)
            total = total.astype(BF16).reshape(4, BLK, high - low)
            if low:
                turn[...] = total
            elif j == 0:
                keep_a[0] = total
            elif j == 2:
                send_a[0] = total
            else:
                first, other = (keep_a, send_a) if j == 1 else (send_a, keep_a)
                first[1, :, :, :SUB] = total[:, :, :SUB]
                other[1, :, :, SUB:] = total[:, :, SUB:]
        for k in range(4):
            tx = (x + k) % 4
            total = turn[(tx % 2) * 2 + tx // 2]
            if k == 0:
                keep_b[0, group] = total
            elif k == 2:
                send_b[0, group] = total
            else:
                first, other = (keep_b, send_b) if k == 1 else (send_b, keep_b)
                first[1, group, :, :SUB] = total[:, :SUB]
                other[1, group, :, SUB:] = total[:, SUB:]

    wgrad_group(z, 0)
    for j, step in enumerate(STEPS):
        for part in range(2):
            block = block_at(part, True, step)
            arrived(part, block)
            onward(part, block, j + 1)
            to_sibling(part, block)
        wgrad_group((z + j + 1) % 4, j + 1)
    halo.relay(0)
    stores = []
    for j, (src, dst) in enumerate(((keep_a, keep_a_out), (send_a, send_a_out),
                                    (keep_b, keep_b_out), (send_b, send_b_out))):
        stores.append(pltpu.make_async_copy(src, dst, store_sem.at[j]))
        stores[-1].start()

    def far_block(part, step, inner):
        if part == 0:
            return block_of((z + step) % 4, (x + inner) % 4)
        return block_of((z + inner) % 4, (x + step) % 4)

    for j, inner in enumerate((0,) + STEPS):
        for step in (1, 3):
            for part in range(2):
                block = far_block(part, step, inner)
                arrived(part, block)
                pass_on(part, block, j, step)
                to_sibling(part, block)
        if j:
            halo.relay(j)
    for inner in (0,) + STEPS:
        for part in range(2):
            block = far_block(part, 2, inner)
            arrived_late(part, block)
            to_sibling(part, block)

    for step in (0,) + STEPS:
        group = (z + step) % 4
        for inner in range(4):
            block = group * 4 + inner
            for part in range(2):
                remote(piece(1 - c, block, part), piece(1 - c, block, part),
                       sib_send.at[part, block], sib_recv.at[part, block], sib).wait_recv()
        feats = pl.ds(pl.multiple_of(group * 4 * BLK, 4 * BLK), 4 * BLK)

        def project(i, carry):
            rows = pl.ds(pl.multiple_of(i * 256, 256), 256)
            total = jnp.zeros((256, 4 * BLK), F32)
            for h in range(2):
                weight = full[h, pl.ds(group * 4, 4)].reshape(4 * BLK, HALF)
                total += lax.dot_general(og[rows, h * HALF:(h + 1) * HALF], weight, NT,
                                         preferred_element_type=F32)
            d_attn[rows, feats] = total.astype(BF16)
            return carry

        lax.fori_loop(0, TOK // 256, project, 0)
        stores.append(pltpu.make_async_copy(d_attn.at[:, feats], d_attn_out.at[:, feats],
                                            store_sem.at[4 + step]))
        stores[-1].start()
    halo.wait()
    for copy in stores:
        copy.wait()
    for copy in exchange:
        copy.wait_send()
    for copy in pending:
        copy.wait_send()


def scatter_kernel(
    to_prev, to_next, keep_a_in, got_a_in, keep_b_in, got_b_in,
    out, from_next, from_prev,
    keep_a, got_a, keep_b, got_b, pass_a, pass_b, more_a, more_b,
    sum_a, sum_b, got_a2, got_b2, packed, last,
    first_send, first_recv, second_send, second_recv, last_send, last_recv,
    load_sem, *halo_sems,
):
    z, x, y, c = place()
    slot = y * 2 + c
    (low_a, high_a), (low_b, high_b) = SUM_PARTS
    loads = []
    for j, (src, dst) in enumerate(((keep_a_in, keep_a), (got_a_in, got_a),
                                    (keep_b_in, keep_b), (got_b_in, got_b))):
        loads.append(pltpu.make_async_copy(src, dst, load_sem.at[j]))
        loads[-1].start()
    greet(z, x, y, c)
    halo = Halo((to_next.at[0], to_next.at[1]), (to_prev.at[0], to_prev.at[1]),
                from_prev, from_next, *halo_sems)
    for copy in loads:
        copy.wait()
    first = []
    for part, (keep, got, ready, more) in enumerate(
            ((keep_a, got_a, pass_a, more_a), (keep_b, got_b, pass_b, more_b))):
        for j in range(4):
            ready[j] = (keep[1, j].astype(F32) + got[1, j].astype(F32)).astype(BF16)
        for i, (cols, step) in enumerate(((slice(0, SUB), 1), (slice(SUB, 2 * SUB), 3))):
            target = device(z, (x + step) % 4, y, c) if part else device((z + step) % 4, x, y, c)
            copy = remote(ready.at[:, :, cols], more.at[:, :, cols], first_send.at[part, i],
                          first_recv.at[part, i], target)
            copy.start()
            first.append(copy)
    halo.start()
    for copy in first:
        copy.wait_recv()
    for keep, got, more, total_ref in (
            (keep_a, got_a, more_a, sum_a), (keep_b, got_b, more_b, sum_b)):
        for j in range(4):
            total = keep[0, j].astype(F32) + got[0, j].astype(F32) + more[j].astype(F32)
            total_ref[j] = total.astype(BF16)
    xs = (x % 2) * 2 + x // 2
    second = []
    for i, step in enumerate(STEPS):
        tz, tx = (z + step) % 4, (x + step) % 4
        for part, src, dst, target in (
            (0, sum_a.at[(tx % 2) * 2 + tx // 2], got_a2.at[i], device(z, tx, y, c)),
            (1, sum_b.at[tz], got_b2.at[i], device(tz, x, y, c)),
        ):
            copy = remote(src, dst, second_send.at[part, i], second_recv.at[part, i], target)
            copy.start()
            second.append(copy)
    halo.relay(0, 1)
    for copy in second:
        copy.wait_recv()
    row = lax.broadcasted_iota(jnp.int32, (8 * PAD, BLK), 0)
    col = lax.broadcasted_iota(jnp.int32, (8 * PAD, BLK), 1)
    spread = jnp.where(
        (col == (row // PAD) * ROWS + row % PAD) & (row % PAD < ROWS), 1.0, 0.0).astype(BF16)
    total_a = sum_a[xs].astype(F32)
    total_b = sum_b[z].astype(F32)
    for i in range(3):
        total_a += got_a2[i].astype(F32)
        total_b += got_b2[i].astype(F32)
    packed[:, :, low_a:high_a] = jnp.dot(spread, total_a.astype(BF16), preferred_element_type=F32).astype(
        BF16).reshape(8, PAD, high_a - low_a)
    packed[:, :, low_b:high_b] = jnp.dot(spread, total_b.astype(BF16), preferred_element_type=F32).astype(
        BF16).reshape(8, PAD, high_b - low_b)
    number = 0
    third = []
    for dy in range(4):
        for dc in range(2):
            if dy or dc:
                ty, tc = (y + dy) % 4, (c + dc) % 2
                copy = remote(packed.at[ty * 2 + tc], last.at[slot], last_send.at[number],
                              last_recv.at[slot], device(z, x, ty, tc))
                copy.start()
                third.append(copy)
                number += 1
    halo.relay(2, 3)
    last[slot] = packed[slot]
    for dy in range(4):
        for dc in range(2):
            if dy or dc:
                src = ((y + dy) % 4) * 2 + (c + dc) % 2
                remote(packed.at[src], last.at[src], last_send.at[0], last_recv.at[src],
                       device(z, x, y, 1 - c)).wait_recv()
    for h in range(2):
        total = last[h].astype(F32)
        for i in range(1, 4):
            total += last[2 * i + h].astype(F32)
        out[:, h * HALF:(h + 1) * HALF] = total[:ROWS] * (1.0 / 256.0)
    halo.wait()
    for copy in first + second + third:
        copy.wait_send()


def attention_kernel(
    first, coords, extents,
    q_all, k_all, v_all, kp_all, vp_all, kn_all, vn_all, a_all, o_all, lse_all, *refs,
):
    outputs, (table, row_s, dqt_s) = refs[-8:-3], refs[-3:]
    begin = first + pl.program_id(0) * GROUP
    frame = lax.axis_index("ctx")

    @pl.when(begin == first)
    def _():
        for k in range(3):
            base = jnp.clip(frame + k - 1, 0, 15) * 4
            for t in range(4):
                r, col = coords[base + t, 1], coords[base + t, 2]
                table[0, k, r * 2 + col] = t
                table[1, k, col * 2 + r] = t

    def one_head(j, carry):
        cols = pl.ds(pl.multiple_of(j * HEAD, HEAD), HEAD)
        flat = [ref.at[:, cols] for ref in (
            q_all, k_all, v_all, kp_all, vp_all, kn_all, vn_all, a_all, o_all) + outputs[:3]]
        sides = [ref.at[:, :, cols] for ref in outputs[3:]]
        head_kernel(begin + j, frame, extents, *flat[:9], lse_all.at[j], *flat[9:], *sides,
                    table, row_s, dqt_s)
        return carry

    lax.fori_loop(0, GROUP, one_head, 0)


def head_kernel(
    head, frame, extents,
    q_ref, k_ref, v_ref, kp_ref, vp_ref, kn_ref, vn_ref, a_ref, o_ref, lse_ref,
    dq_ref, dk_ref, dv_ref, prev_ref, next_ref, table, row_s, dqt_s,
):
    scale = HEAD ** (-0.5)
    near_f, near_r, near_c = extents[head, 0], extents[head, 1], extents[head, 2]
    order = jnp.where(near_c == 0, 1, 0)
    keys, vals = (kp_ref, k_ref, kn_ref), (vp_ref, v_ref, vn_ref)
    outs = ((prev_ref.at[0], prev_ref.at[1]), (dk_ref, dv_ref), (next_ref.at[0], next_ref.at[1]))

    def spot(k, s):
        return pl.ds(pl.multiple_of(table[order, k, s] * TILE, TILE), TILE)

    def rows_of(ref, k, begin, size, whole):
        if whole:
            return ref[begin:begin + size, :]
        tiles = [ref[spot(k, s), :] for s in range(begin // TILE, (begin + size) // TILE)]
        return tiles[0] if len(tiles) == 1 else jnp.concatenate(tiles, axis=0)

    def line_of(i, begin, size, whole):
        if whole:
            return row_s[i:i + 1, begin:begin + size]
        tiles = [row_s[i:i + 1, spot(1, s)] for s in range(begin // TILE, (begin + size) // TILE)]
        return tiles[0] if len(tiles) == 1 else jnp.concatenate(tiles, axis=1)

    def frame_of(k, size):
        whole = size == TOK
        step = min(size, 256)
        queries = [
            (rows_of(q_ref, 1, at, size, whole), rows_of(a_ref, 1, at, size, whole),
             line_of(0, at, size, whole), line_of(1, at, size, whole))
            for at in range(0, TOK, size)]
        units = [(g, at) for g in range(TOK // size) for at in range(g * size, (g + 1) * size, step)]
        ready = []
        for g, at in units:
            q, a, lse, delta = queries[g]
            key = rows_of(keys[k], k, at, step, whole)
            scores = lax.dot_general(key, q, NT, preferred_element_type=F32)
            d_probs = lax.dot_general(rows_of(vals[k], k, at, step, whole), a, NT,
                                      preferred_element_type=F32)
            ready.append((key, scores, d_probs))
        halves = []
        for (g, at), (key, scores, d_probs) in zip(units, ready):
            q, a, lse, delta = queries[g]
            probs = jnp.exp2(scores * (scale * LOG2E) - lse)
            halves.append((probs.astype(BF16), (probs * (d_probs - delta)).astype(BF16)))
        sums = [None] * (TOK // size)
        for (g, at), (key, _, _), (probs, d_scores) in zip(units, ready, halves):
            q, a, lse, delta = queries[g]
            dv = jnp.dot(probs, a, preferred_element_type=F32)
            dk = jnp.dot(d_scores, q, preferred_element_type=F32) * scale
            dqt = jnp.dot(key.T, d_scores, preferred_element_type=F32)
            sums[g] = dqt if sums[g] is None else sums[g] + dqt
            for ref, value in zip(outs[k], (dk, dv)):
                if whole:
                    ref[at:at + step, :] = value.astype(ref.dtype)
                else:
                    for i in range(step // TILE):
                        ref[spot(k, at // TILE + i), :] = value[i * TILE:(i + 1) * TILE].astype(
                            ref.dtype)
        for g, total in enumerate(sums):
            span = slice(g * size, (g + 1) * size)
            if k == 1:
                dqt_s[:, span] = total
            else:
                dqt_s[:, span] += total

    wide = near_r * near_c == 1
    modes = ((TOK, wide), (256, near_r + near_c == 1), (TILE, near_r + near_c == 0))
    ones = jnp.ones((8, HEAD), BF16)
    prod = a_ref[...].astype(F32) * o_ref[...].astype(F32)
    high = prod.astype(BF16)
    low = (prod - high.astype(F32)).astype(BF16)
    delta = lax.dot_general(ones, high, NT, preferred_element_type=F32)
    delta += lax.dot_general(ones, low, NT, preferred_element_type=F32)
    row_s[0:1, :] = lse_ref[...] * LOG2E
    row_s[1:2, :] = delta[0:1]
    for size, here in modes:
        @pl.when(here)
        def _():
            frame_of(1, size)

    for k, there, ref in ((0, frame > 0, prev_ref), (2, frame < 15, next_ref)):
        use = (near_f == 1) & there
        for size, here in modes:
            @pl.when(use & here)
            def _():
                frame_of(k, size)

        @pl.when(jnp.logical_not(use))
        def _():
            ref[...] = jnp.zeros_like(ref)

    @pl.when(wide)
    def _():
        dq_ref[...] = (dqt_s[...].T * scale).astype(BF16)

    @pl.when(jnp.logical_not(wide))
    def _():
        for s in range(4):
            dq_ref[spot(1, s), :] = (dqt_s[:, s * TILE:(s + 1) * TILE].T * scale).astype(BF16)


def combine_kernel(dk, dv, ahead0, behind0, ahead1, behind1, key_out, value_out):
    step = pl.program_id(0)
    frame = lax.axis_index("ctx")

    def put(ahead, behind):
        for i, (own, out) in enumerate(((dk, key_out), (dv, value_out))):
            total = own[...] + jnp.where(frame < 15, ahead[i].astype(F32), 0.0)
            total += jnp.where(frame > 0, behind[i].astype(F32), 0.0)
            out[...] = total.astype(BF16)

    @pl.when(step < 2)
    def _():
        put(ahead0, behind0)

    @pl.when(step >= 2)
    def _():
        put(ahead1, behind1)


def any_spec():
    return pl.BlockSpec(memory_space=pl.ANY)


def vmem_spec():
    return pl.BlockSpec(memory_space=pltpu.VMEM)


def along_x(value, step):
    pairs = []
    for dp in range(8):
        for ctx in range(16):
            x = (ctx // 8) * 2 + dp % 2
            tx = (x + step) % 4
            pairs.append((dp * 16 + ctx, ((dp // 2) * 2 + tx % 2) * 16 + (tx // 2) * 8 + ctx % 8))
    return lax.ppermute(value, ("dp", "ctx"), pairs)


def along_z(value, step):
    return lax.ppermute(value, "dp", [(i, (i + 2 * step) % 8) for i in range(8)])


def shards(
    queries, key_rows, values, saved_out, log_sum, out_grad, out_weight, tile_coords, extents
):
    q, k, v, so, og = (a[0] for a in (queries, key_rows, values, saved_out, out_grad))
    pair = jax.ShapeDtypeStruct((2, TOK, HD), BF16)
    dma = pltpu.SemaphoreType.DMA
    moving = jax.ShapeDtypeStruct((2, 4, BLK, SUM_CUT), BF16)
    before, after, d_attn, keep_a, send_a, keep_b, send_b = pl.pallas_call(
        gather_kernel,
        out_shape=(pair, pair, jax.ShapeDtypeStruct((TOK, HD), BF16)) + (moving,) * 4,
        in_specs=[vmem_spec()] + [any_spec()] * 4,
        out_specs=(any_spec(),) * 7,
        scratch_shapes=[
            pltpu.VMEM((2, PAD, HALF), BF16),
            pltpu.VMEM((8, PAD, HALF), BF16),
            pltpu.VMEM((2, 16, BLK, HALF), BF16),
            pltpu.VMEM((TOK, HD), BF16),
            pltpu.VMEM((TOK, D), BF16),
            pltpu.VMEM((TOK, HD), BF16),
            pltpu.VMEM((TOK, HALF), BF16),
            pltpu.VMEM((4, BLK, SUM_CUT), BF16),
            pltpu.VMEM((TOK, HD), BF16),
        ] + [pltpu.VMEM((2, 4, BLK, SUM_CUT), BF16)] * 4 + [
            dma((7,)), dma((8,)), dma((2, 3)), dma((2, 4, 2)), dma((2, 4, 2)), dma((2, 16)),
            dma((2, 16)), dma((2, 16)), dma((2, 16)), dma((2,)), dma((2,)), dma((2,)), dma((8,)),
        ] + HALO_SEMS,
        compiler_params=pltpu.CompilerParams(
            collective_id=0, has_side_effects=True, vmem_limit_bytes=VMEM_LIMIT),
        cost_estimate=pl.CostEstimate(
            flops=10**10, bytes_accessed=20 * 10**6, transcendentals=0),
        name="gather",
    )(out_weight, k, v, so, og)
    got_a, got_b = along_z(send_a, 2), along_x(send_b, 2)

    own32 = jax.ShapeDtypeStruct((TOK, HD), F32)
    own16 = jax.ShapeDtypeStruct((TOK, HD), BF16)
    half_pair = jax.ShapeDtypeStruct((2, TOK, HD // 2), BF16)
    grads, towards = (), []
    for first in (0, H // 2):
        skip, wide = first // GROUP, GROUP * HEAD
        col = pl.BlockSpec((TOK, wide), lambda h, *_, skip=skip: (0, skip + h))
        row = pl.BlockSpec((GROUP, 1, TOK), lambda h, *_, skip=skip: (skip + h, 0, 0))
        sides = pl.BlockSpec((2, TOK, wide), lambda h, *_: (0, 0, h))
        k_side = pl.BlockSpec((None, TOK, wide), lambda h, *_, skip=skip: (0, 0, skip + h))
        v_side = pl.BlockSpec((None, TOK, wide), lambda h, *_, skip=skip: (1, 0, skip + h))
        *grads, to_prev, to_next = pl.pallas_call(
            functools.partial(attention_kernel, first),
            out_shape=(own16, own32, own32, half_pair, half_pair),
            grid_spec=pltpu.PrefetchScalarGridSpec(
                num_scalar_prefetch=2,
                grid=(H // 2 // GROUP,),
                in_specs=[col] * 3 + [k_side, v_side] * 2 + [col] * 2 + [row]
                + [any_spec()] * len(grads),
                out_specs=(col,) * 3 + (sides,) * 2,
                scratch_shapes=[
                    pltpu.SMEM((2, 3, 4), jnp.int32),
                    pltpu.VMEM((8, TOK), F32),
                    pltpu.VMEM((HEAD, TOK), F32),
                ],
            ),
            input_output_aliases={12 + i: i for i in range(len(grads))},
            compiler_params=pltpu.CompilerParams(vmem_limit_bytes=VMEM_LIMIT),
            cost_estimate=pl.CostEstimate(
                flops=6 * 10**9, bytes_accessed=15 * 10**6, transcendentals=5 * 10**6),
            name="attention",
        )(tile_coords, extents, q, k, v, before, before, after, after, d_attn, so,
          log_sum[0][:, None, :], *grads)
        towards.append((to_prev, to_next))
    dq, dk, dv = grads
    ahead = lax.ppermute(towards[0][0], "ctx", [(i + 1, i) for i in range(15)])
    behind = lax.ppermute(towards[0][1], "ctx", [(i, i + 1) for i in range(15)])

    weight_grad, from_next, from_prev = pl.pallas_call(
        scatter_kernel,
        out_shape=(jax.ShapeDtypeStruct((ROWS, D), F32), half_pair, half_pair),
        in_specs=[any_spec()] * 6,
        out_specs=(vmem_spec(), any_spec(), any_spec()),
        scratch_shapes=[pltpu.VMEM((2, 4, BLK, SUM_CUT), BF16)] * 4
        + [pltpu.VMEM((4, BLK, SUM_CUT), BF16)] * 6
        + [pltpu.VMEM((3, BLK, SUM_CUT), BF16)] * 2 + [
            pltpu.VMEM((8, PAD, HALF), BF16),
            pltpu.VMEM((8, PAD, HALF), BF16),
            dma((2, 2)), dma((2, 2)), dma((2, 3)), dma((2, 3)), dma((7,)), dma((8,)),
            dma((4,)),
        ] + HALO_SEMS,
        compiler_params=pltpu.CompilerParams(
            collective_id=1, has_side_effects=True, vmem_limit_bytes=VMEM_LIMIT),
        cost_estimate=pl.CostEstimate(
            flops=10**10, bytes_accessed=20 * 10**6, transcendentals=0),
        name="scatter",
    )(*towards[1], keep_a, got_a, keep_b, got_b)

    wide = HD // 4
    whole = pl.BlockSpec((TOK, wide), lambda i: (0, i))
    lower = pl.BlockSpec((2, TOK, wide), lambda i: (0, 0, jnp.minimum(i, 1)))
    upper = pl.BlockSpec((2, TOK, wide), lambda i: (0, 0, jnp.maximum(i - 2, 0)))
    key_grad, value_grad = pl.pallas_call(
        combine_kernel,
        out_shape=(own16, own16),
        grid=(4,),
        in_specs=[whole, whole, lower, lower, upper, upper],
        out_specs=(whole, whole),
        compiler_params=pltpu.CompilerParams(vmem_limit_bytes=VMEM_LIMIT),
        name="combine",
    )(dk, dv, ahead, behind, from_next, from_prev)
    return dq[None], key_grad[None], value_grad[None], weight_grad


def solution(mesh):
    return jax.shard_map(
        shards,
        mesh=mesh,
        in_specs=(
            P("dp", "ctx", None),
            P("dp", "ctx", None),
            P("dp", "ctx", None),
            P("dp", "ctx", None),
            P("dp", None, "ctx"),
            P("dp", "ctx", None),
            P(("dp", "ctx"), None),
            P(),
            P(),
        ),
        out_specs=(
            P("dp", "ctx", None),
            P("dp", "ctx", None),
            P("dp", "ctx", None),
            P(("dp", "ctx"), None),
        ),
        check_vma=False,
    )
```

```python
import functools
import functools
import math

import jax
import jax.numpy as jnp
from jax import lax
from jax.experimental import pallas as pl
from jax.experimental.pallas import tpu as pltpu
from jax.sharding import PartitionSpec as P

H = 12
HEAD = 128
TILE = 128
TOK = 512
HD = 1536
D = 3072
HALF = D // 2
ROWS = 12
PAD = 16
BLK = 8 * ROWS
CUT = 1024
PARTS = ((0, CUT), (CUT, HALF))
SUM_CUT = 768
SUM_PARTS = ((0, SUM_CUT), (SUM_CUT, HALF))
SUB = SUM_CUT // 2
STEPS = (1, 3, 2)
GROUP = 2
VMEM_LIMIT = 60 * 2**20
MESH = pl.DeviceIdType.MESH
F32 = jnp.float32
BF16 = jnp.bfloat16
LOG2E = math.log2(math.e)
NT = (((1,), (1,)), ((), ()))
TN = (((0,), (0,)), ((), ()))


def place():
    dp, ctx = lax.axis_index("dp"), lax.axis_index("ctx")
    return dp // 2, (ctx // 8) * 2 + dp % 2, (ctx // 2) % 4, ctx % 2


def device(z, x, y, c):
    return (z * 2 + x % 2, (x // 2) * 8 + y * 2 + c)


def block_of(z, x):
    return z * 4 + (x % 2) * 2 + x // 2


def remote(src, dst, send, recv, target):
    return pltpu.make_async_remote_copy(
        src_ref=src, dst_ref=dst, send_sem=send, recv_sem=recv,
        device_id=target, device_id_type=MESH,
    )


def greet(z, x, y, c):
    barrier = pltpu.get_barrier_semaphore()

    def tell(target):
        pl.semaphore_signal(barrier, inc=1, device_id=target, device_id_type=MESH)

    for dy in range(4):
        for dc in range(2):
            if dy or dc:
                tell(device(z, x, (y + dy) % 4, (c + dc) % 2))
    for step in STEPS:
        tell(device(z, (x + step) % 4, y, c))
        tell(device((z + step) % 4, x, y, c))

    ctx, dp = lax.axis_index("ctx"), lax.axis_index("dp")

    @pl.when(ctx == 7)
    def _():
        tell((dp, ctx + 1))

    @pl.when(ctx == 8)
    def _():
        tell((dp, ctx - 1))

    pl.semaphore_wait(barrier, 13 + jnp.where((ctx == 7) | (ctx == 8), 1, 0))


HALO_SEMS = [pltpu.SemaphoreType.DMA(shape) for shape in ((2,), (2,), (2, 4), (2, 4), (2, 4))]


class Halo:
    def __init__(self, ups, downs, before, after, send, recv, piece_send, piece_recv, relay_send):
        self.dp, self.ctx = lax.axis_index("dp"), lax.axis_index("ctx")
        ctx = self.ctx
        ways = (
            (ups, before, jnp.minimum(ctx + 1, 15), jnp.where(ctx == 7, 0, jnp.minimum(ctx + 1, 15)), 8),
            (downs, after, jnp.maximum(ctx - 1, 0), jnp.where(ctx == 8, 15, jnp.maximum(ctx - 1, 0)), 7),
        )
        self.straight, self.pieces, self.relays = [], [], []
        for i, (src, dst, near, first, last) in enumerate(ways):
            self.straight.append(
                remote(src[0], dst.at[0], send.at[i], recv.at[i], (self.dp, near)))
            spans = [pl.ds(j * TILE, TILE) for j in range(TOK // TILE)]
            self.pieces.append([
                remote(src[1].at[span], dst.at[1, span], piece_send.at[i, j], piece_recv.at[i, j],
                       (self.dp, first)) for j, span in enumerate(spans)])
            self.relays.append([
                remote(dst.at[1, span], dst.at[1, span], relay_send.at[i, j], piece_recv.at[i, j],
                       (self.dp, last)) for j, span in enumerate(spans)])
        self.sends = (ctx < 15, ctx > 0)
        self.gets = (ctx > 0, ctx < 15)
        self.passes = (ctx == 0, ctx == 15)
        self.far = (ctx == 7, ctx == 8)

    def start(self):
        for i in range(2):
            @pl.when(self.sends[i])
            def _():
                for copy in self.pieces[i]:
                    copy.start()

            @pl.when(self.sends[i] & jnp.logical_not(self.far[i]))
            def _():
                self.straight[i].start()

    def start_far(self):
        for i in range(2):
            @pl.when(self.far[i])
            def _():
                self.straight[i].start()

    def relay(self, *numbers):
        for i in range(2):
            @pl.when(self.passes[i])
            def _():
                for j in numbers:
                    self.pieces[i][j].wait_recv()
                    self.relays[i][j].start()

    def wait(self):
        for i in range(2):
            @pl.when(self.gets[i])
            def _():
                self.straight[i].wait_recv()
                for copy in self.pieces[i]:
                    copy.wait_recv()

            @pl.when(self.sends[i])
            def _():
                self.straight[i].wait_send()
                for copy in self.pieces[i]:
                    copy.wait_send()

            @pl.when(self.passes[i])
            def _():
                for onward in self.relays[i]:
                    onward.wait_send()


def gather_kernel(
    strip, keys, vals, so_hbm, og_hbm,
    before, after, d_attn_out, keep_a_out, send_a_out, keep_b_out, send_b_out,
    padded, strips, full, so, og, so_sib, og_sib, turn, d_attn, keep_a, send_a, keep_b, send_b,
    strip_send, strip_recv, near_send, far_send, pass_send, ag_recv, late_recv, sib_send, sib_recv,
    ex_send, ex_recv, load_sem, store_sem, *halo_sems,
):
    z, x, y, c = place()
    sib = device(z, x, y, 1 - c)
    me = block_of(z, x)
    slot = y * 2 + c
    loads = [pltpu.make_async_copy(so_hbm, so, load_sem.at[0]),
             pltpu.make_async_copy(og_hbm, og, load_sem.at[1])]
    for copy in loads:
        copy.start()
    for h in range(2):
        padded[h, 0:ROWS] = strip[:, h * HALF:(h + 1) * HALF]
        padded[h, ROWS:PAD] = jnp.zeros((PAD - ROWS, HALF), BF16)
    strips[slot] = padded[c]
    greet(z, x, y, c)

    pending = []
    number = 0
    for dy in range(4):
        for dc in range(2):
            if dy or dc:
                tc = (c + dc) % 2
                copy = remote(padded.at[tc], strips.at[slot], strip_send.at[number],
                              strip_recv.at[slot], device(z, x, (y + dy) % 4, tc))
                copy.start()
                pending.append(copy)
                number += 1
    other = pl.ds(pl.multiple_of((1 - c) * HALF, HALF), HALF)
    exchange = [
        remote(so_hbm, so_sib, ex_send.at[0], ex_recv.at[0], sib),
        remote(og_hbm.at[:, other], og_sib, ex_send.at[1], ex_recv.at[1], sib),
    ]
    for copy in exchange:
        copy.start()
    for dy in range(4):
        for dc in range(2):
            if dy or dc:
                src = ((y + dy) % 4) * 2 + (c + dc) % 2
                remote(strips.at[src], strips.at[src], strip_send.at[0], strip_recv.at[src],
                       sib).wait_recv()
    row = lax.broadcasted_iota(jnp.int32, (BLK, 8 * PAD), 0)
    col = lax.broadcasted_iota(jnp.int32, (BLK, 8 * PAD), 1)
    pick = jnp.where(col == (row // ROWS) * PAD + row % ROWS, 1.0, 0.0).astype(BF16)
    for o in range(0, HALF, 768):
        full[c, me, :, o:o + 768] = jnp.dot(
            pick, strips[:, :, o:o + 768].reshape(8 * PAD, 768),
            preferred_element_type=F32).astype(BF16)

    def piece(half, block, part):
        low, high = PARTS[part]
        return full.at[half, block, :, low:high]

    def along(part, first, step):
        over_x = (part == 0) == first
        return device(z, (x + step) % 4, y, c) if over_x else device((z + step) % 4, x, y, c)

    def block_at(part, first, step):
        if part == 0:
            return block_of(z, (x + step) % 4)
        return block_of((z + step) % 4, x)

    for part in range(2):
        for i, step in enumerate(STEPS):
            copy = remote(piece(c, me, part), piece(c, me, part), near_send.at[part, i],
                          ag_recv.at[part, me], along(part, True, step))
            copy.start()
            pending.append(copy)

    def onward(part, block, j):
        for i, step in enumerate((1, 3)):
            copy = remote(piece(c, block, part), piece(c, block, part), far_send.at[part, j, i],
                          ag_recv.at[part, block], along(part, False, step))
            copy.start()
            pending.append(copy)

    def half_piece(block, part, upper):
        low, high = PARTS[part]
        return full.at[c, block, (BLK // 2 if upper else 0):(BLK if upper else BLK // 2), low:high]

    def pass_on(part, block, j, step):
        upper = step == 1
        copy = remote(half_piece(block, part, upper), half_piece(block, part, upper),
                      pass_send.at[part, j, int(upper)],
                      (late_recv if upper else ag_recv).at[part, block],
                      along(part, False, 4 - step))
        copy.start()
        pending.append(copy)

    def arrived_late(part, block):
        for upper, sem in ((False, ag_recv), (True, late_recv)):
            remote(half_piece(block, part, upper), half_piece(block, part, upper),
                   near_send.at[part, 0], sem.at[part, block], sib).wait_recv()

    def to_sibling(part, block):
        copy = remote(piece(c, block, part), piece(c, block, part), sib_send.at[part, block],
                      sib_recv.at[part, block], sib)
        copy.start()
        pending.append(copy)

    def arrived(part, block):
        remote(piece(c, block, part), piece(c, block, part), near_send.at[part, 0],
               ag_recv.at[part, block], sib).wait_recv()

    for part in range(2):
        onward(part, me, 0)
        to_sibling(part, me)

    halo = Halo((keys, vals), (keys, vals), before, after, *halo_sems)
    halo.start()
    for copy in exchange:
        copy.wait_recv()
    for copy in loads:
        copy.wait()
    def wgrad_group(group, j):
        rows = pl.ds(pl.multiple_of(group * 4 * BLK, 4 * BLK), 4 * BLK)
        for low, high in SUM_PARTS:
            cols = pl.ds(pl.multiple_of(c * HALF + low, 128), high - low)
            total = lax.dot_general(so[:, rows], og[:, cols], TN, preferred_element_type=F32)
            total += lax.dot_general(so_sib[:, rows], og_sib[:, low:high], TN,
                                     preferred_element_type=F32)
            total = total.astype(BF16).reshape(4, BLK, high - low)
            if low:
                turn[...] = total
            elif j == 0:
                keep_a[0] = total
            elif j == 2:
                send_a[0] = total
            else:
                first, other = (keep_a, send_a) if j == 1 else (send_a, keep_a)
                first[1, :, :, :SUB] = total[:, :, :SUB]
                other[1, :, :, SUB:] = total[:, :, SUB:]
        for k in range(4):
            tx = (x + k) % 4
            total = turn[(tx % 2) * 2 + tx // 2]
            if k == 0:
                keep_b[0, group] = total
            elif k == 2:
                send_b[0, group] = total
            else:
                first, other = (keep_b, send_b) if k == 1 else (send_b, keep_b)
                first[1, group, :, :SUB] = total[:, :SUB]
                other[1, group, :, SUB:] = total[:, SUB:]

    wgrad_group(z, 0)
    for j, step in enumerate(STEPS):
        for part in range(2):
            block = block_at(part, True, step)
            arrived(part, block)
            onward(part, block, j + 1)
            to_sibling(part, block)
        wgrad_group((z + j + 1) % 4, j + 1)
    halo.start_far()
    halo.relay(0)
    stores = []
    for j, (src, dst) in enumerate(((keep_a, keep_a_out), (send_a, send_a_out),
                                    (keep_b, keep_b_out), (send_b, send_b_out))):
        stores.append(pltpu.make_async_copy(src, dst, store_sem.at[j]))
        stores[-1].start()

    def far_block(part, step, inner):
        if part == 0:
            return block_of((z + step) % 4, (x + inner) % 4)
        return block_of((z + inner) % 4, (x + step) % 4)

    for j, inner in enumerate((0,) + STEPS):
        for step in (1, 3):
            for part in range(2):
                block = far_block(part, step, inner)
                arrived(part, block)
                pass_on(part, block, j, step)
                to_sibling(part, block)
        if j:
            halo.relay(j)
    for inner in (0,) + STEPS:
        for part in range(2):
            block = far_block(part, 2, inner)
            arrived_late(part, block)
            to_sibling(part, block)

    for step in (0,) + STEPS:
        group = (z + step) % 4
        for inner in range(4):
            block = group * 4 + inner
            for part in range(2):
                remote(piece(1 - c, block, part), piece(1 - c, block, part),
                       sib_send.at[part, block], sib_recv.at[part, block], sib).wait_recv()
        feats = pl.ds(pl.multiple_of(group * 4 * BLK, 4 * BLK), 4 * BLK)

        def project(i, carry):
            rows = pl.ds(pl.multiple_of(i * 256, 256), 256)
            total = jnp.zeros((256, 4 * BLK), F32)
            for h in range(2):
                weight = full[h, pl.ds(group * 4, 4)].reshape(4 * BLK, HALF)
                total += lax.dot_general(og[rows, h * HALF:(h + 1) * HALF], weight, NT,
                                         preferred_element_type=F32)
            d_attn[rows, feats] = total.astype(BF16)
            return carry

        lax.fori_loop(0, TOK // 256, project, 0)
        stores.append(pltpu.make_async_copy(d_attn.at[:, feats], d_attn_out.at[:, feats],
                                            store_sem.at[4 + step]))
        stores[-1].start()
    halo.wait()
    for copy in stores:
        copy.wait()
    for copy in exchange:
        copy.wait_send()
    for copy in pending:
        copy.wait_send()


def scatter_kernel(
    to_prev, to_next, keep_a_in, got_a_in, keep_b_in, got_b_in,
    out, from_next, from_prev,
    keep_a, got_a, keep_b, got_b, pass_a, pass_b, more_a, more_b,
    sum_a, sum_b, got_a2, got_b2, packed, last,
    first_send, first_recv, second_send, second_recv, last_send, last_recv,
    load_sem, *halo_sems,
):
    z, x, y, c = place()
    slot = y * 2 + c
    (low_a, high_a), (low_b, high_b) = SUM_PARTS
    loads = []
    for j, (src, dst) in enumerate(((keep_a_in, keep_a), (got_a_in, got_a),
                                    (keep_b_in, keep_b), (got_b_in, got_b))):
        loads.append(pltpu.make_async_copy(src, dst, load_sem.at[j]))
        loads[-1].start()
    greet(z, x, y, c)
    halo = Halo((to_next.at[0], to_next.at[1]), (to_prev.at[0], to_prev.at[1]),
                from_prev, from_next, *halo_sems)
    for copy in loads:
        copy.wait()
    first = []
    for part, (keep, got, ready, more) in enumerate(
            ((keep_a, got_a, pass_a, more_a), (keep_b, got_b, pass_b, more_b))):
        for j in range(4):
            ready[j] = (keep[1, j].astype(F32) + got[1, j].astype(F32)).astype(BF16)
        for i, (cols, step) in enumerate(((slice(0, SUB), 1), (slice(SUB, 2 * SUB), 3))):
            target = device(z, (x + step) % 4, y, c) if part else device((z + step) % 4, x, y, c)
            copy = remote(ready.at[:, :, cols], more.at[:, :, cols], first_send.at[part, i],
                          first_recv.at[part, i], target)
            copy.start()
            first.append(copy)
    halo.start()
    halo.start_far()
    for copy in first:
        copy.wait_recv()
    for keep, got, more, total_ref in (
            (keep_a, got_a, more_a, sum_a), (keep_b, got_b, more_b, sum_b)):
        for j in range(4):
            total = keep[0, j].astype(F32) + got[0, j].astype(F32) + more[j].astype(F32)
            total_ref[j] = total.astype(BF16)
    xs = (x % 2) * 2 + x // 2
    second = []
    for i, step in enumerate(STEPS):
        tz, tx = (z + step) % 4, (x + step) % 4
        for part, src, dst, target in (
            (0, sum_a.at[(tx % 2) * 2 + tx // 2], got_a2.at[i], device(z, tx, y, c)),
            (1, sum_b.at[tz], got_b2.at[i], device(tz, x, y, c)),
        ):
            copy = remote(src, dst, second_send.at[part, i], second_recv.at[part, i], target)
            copy.start()
            second.append(copy)
    halo.relay(0, 1)
    for copy in second:
        copy.wait_recv()
    row = lax.broadcasted_iota(jnp.int32, (8 * PAD, BLK), 0)
    col = lax.broadcasted_iota(jnp.int32, (8 * PAD, BLK), 1)
    spread = jnp.where(
        (col == (row // PAD) * ROWS + row % PAD) & (row % PAD < ROWS), 1.0, 0.0).astype(BF16)
    total_a = sum_a[xs].astype(F32)
    total_b = sum_b[z].astype(F32)
    for i in range(3):
        total_a += got_a2[i].astype(F32)
        total_b += got_b2[i].astype(F32)
    packed[:, :, low_a:high_a] = jnp.dot(spread, total_a.astype(BF16), preferred_element_type=F32).astype(
        BF16).reshape(8, PAD, high_a - low_a)
    packed[:, :, low_b:high_b] = jnp.dot(spread, total_b.astype(BF16), preferred_element_type=F32).astype(
        BF16).reshape(8, PAD, high_b - low_b)
    number = 0
    third = []
    for dy in range(4):
        for dc in range(2):
            if dy or dc:
                ty, tc = (y + dy) % 4, (c + dc) % 2
                copy = remote(packed.at[ty * 2 + tc], last.at[slot], last_send.at[number],
                              last_recv.at[slot], device(z, x, ty, tc))
                copy.start()
                third.append(copy)
                number += 1
    halo.relay(2, 3)
    last[slot] = packed[slot]
    for dy in range(4):
        for dc in range(2):
            if dy or dc:
                src = ((y + dy) % 4) * 2 + (c + dc) % 2
                remote(packed.at[src], last.at[src], last_send.at[0], last_recv.at[src],
                       device(z, x, y, 1 - c)).wait_recv()
    for h in range(2):
        total = last[h].astype(F32)
        for i in range(1, 4):
            total += last[2 * i + h].astype(F32)
        out[:, h * HALF:(h + 1) * HALF] = total[:ROWS] * (1.0 / 256.0)
    halo.wait()
    for copy in first + second + third:
        copy.wait_send()


def attention_kernel(
    first, coords, extents,
    q_all, k_all, v_all, kp_all, vp_all, kn_all, vn_all, a_all, o_all, lse_all, *refs,
):
    outputs, (table, row_s, dqt_s) = refs[-8:-3], refs[-3:]
    begin = first + pl.program_id(0) * GROUP
    frame = lax.axis_index("ctx")

    @pl.when(begin == first)
    def _():
        for k in range(3):
            base = jnp.clip(frame + k - 1, 0, 15) * 4
            for t in range(4):
                r, col = coords[base + t, 1], coords[base + t, 2]
                table[0, k, r * 2 + col] = t
                table[1, k, col * 2 + r] = t

    def one_head(j, carry):
        cols = pl.ds(pl.multiple_of(j * HEAD, HEAD), HEAD)
        flat = [ref.at[:, cols] for ref in (
            q_all, k_all, v_all, kp_all, vp_all, kn_all, vn_all, a_all, o_all) + outputs[:3]]
        sides = [ref.at[:, :, cols] for ref in outputs[3:]]
        head_kernel(begin + j, frame, extents, *flat[:9], lse_all.at[j], *flat[9:], *sides,
                    table, row_s, dqt_s)
        return carry

    lax.fori_loop(0, GROUP, one_head, 0)


def head_kernel(
    head, frame, extents,
    q_ref, k_ref, v_ref, kp_ref, vp_ref, kn_ref, vn_ref, a_ref, o_ref, lse_ref,
    dq_ref, dk_ref, dv_ref, prev_ref, next_ref, table, row_s, dqt_s,
):
    scale = HEAD ** (-0.5)
    near_f, near_r, near_c = extents[head, 0], extents[head, 1], extents[head, 2]
    order = jnp.where(near_c == 0, 1, 0)
    keys, vals = (kp_ref, k_ref, kn_ref), (vp_ref, v_ref, vn_ref)
    outs = ((prev_ref.at[0], prev_ref.at[1]), (dk_ref, dv_ref), (next_ref.at[0], next_ref.at[1]))

    def spot(k, s):
        return pl.ds(pl.multiple_of(table[order, k, s] * TILE, TILE), TILE)

    def rows_of(ref, k, begin, size, whole):
        if whole:
            return ref[begin:begin + size, :]
        tiles = [ref[spot(k, s), :] for s in range(begin // TILE, (begin + size) // TILE)]
        return tiles[0] if len(tiles) == 1 else jnp.concatenate(tiles, axis=0)

    def line_of(i, begin, size, whole):
        if whole:
            return row_s[i:i + 1, begin:begin + size]
        tiles = [row_s[i:i + 1, spot(1, s)] for s in range(begin // TILE, (begin + size) // TILE)]
        return tiles[0] if len(tiles) == 1 else jnp.concatenate(tiles, axis=1)

    def frame_of(k, size):
        whole = size == TOK
        step = min(size, 256)
        queries = [
            (rows_of(q_ref, 1, at, size, whole), rows_of(a_ref, 1, at, size, whole),
             line_of(0, at, size, whole), line_of(1, at, size, whole))
            for at in range(0, TOK, size)]
        units = [(g, at) for g in range(TOK // size) for at in range(g * size, (g + 1) * size, step)]
        ready = []
        for g, at in units:
            q, a, lse, delta = queries[g]
            key = rows_of(keys[k], k, at, step, whole)
            scores = lax.dot_general(key, q, NT, preferred_element_type=F32)
            d_probs = lax.dot_general(rows_of(vals[k], k, at, step, whole), a, NT,
                                      preferred_element_type=F32)
            ready.append((key, scores, d_probs))
        halves = []
        for (g, at), (key, scores, d_probs) in zip(units, ready):
            q, a, lse, delta = queries[g]
            probs = jnp.exp2(scores * (scale * LOG2E) - lse)
            halves.append((probs.astype(BF16), (probs * (d_probs - delta)).astype(BF16)))
        sums = [None] * (TOK // size)
        for (g, at), (key, _, _), (probs, d_scores) in zip(units, ready, halves):
            q, a, lse, delta = queries[g]
            dv = jnp.dot(probs, a, preferred_element_type=F32)
            dk = jnp.dot(d_scores, q, preferred_element_type=F32) * scale
            dqt = jnp.dot(key.T, d_scores, preferred_element_type=F32)
            sums[g] = dqt if sums[g] is None else sums[g] + dqt
            for ref, value in zip(outs[k], (dk, dv)):
                if whole:
                    ref[at:at + step, :] = value.astype(ref.dtype)
                else:
                    for i in range(step // TILE):
                        ref[spot(k, at // TILE + i), :] = value[i * TILE:(i + 1) * TILE].astype(
                            ref.dtype)
        for g, total in enumerate(sums):
            span = slice(g * size, (g + 1) * size)
            if k == 1:
                dqt_s[:, span] = total
            else:
                dqt_s[:, span] += total

    wide = near_r * near_c == 1
    modes = ((TOK, wide), (256, near_r + near_c == 1), (TILE, near_r + near_c == 0))
    ones = jnp.ones((8, HEAD), BF16)
    prod = a_ref[...].astype(F32) * o_ref[...].astype(F32)
    high = prod.astype(BF16)
    low = (prod - high.astype(F32)).astype(BF16)
    delta = lax.dot_general(ones, high, NT, preferred_element_type=F32)
    delta += lax.dot_general(ones, low, NT, preferred_element_type=F32)
    row_s[0:1, :] = lse_ref[...] * LOG2E
    row_s[1:2, :] = delta[0:1]
    for size, here in modes:
        @pl.when(here)
        def _():
            frame_of(1, size)

    for k, there, ref in ((0, frame > 0, prev_ref), (2, frame < 15, next_ref)):
        use = (near_f == 1) & there
        for size, here in modes:
            @pl.when(use & here)
            def _():
                frame_of(k, size)

        @pl.when(jnp.logical_not(use))
        def _():
            ref[...] = jnp.zeros_like(ref)

    @pl.when(wide)
    def _():
        dq_ref[...] = (dqt_s[...].T * scale).astype(BF16)

    @pl.when(jnp.logical_not(wide))
    def _():
        for s in range(4):
            dq_ref[spot(1, s), :] = (dqt_s[:, s * TILE:(s + 1) * TILE].T * scale).astype(BF16)


def combine_kernel(dk, dv, ahead0, behind0, ahead1, behind1, key_out, value_out):
    step = pl.program_id(0)
    frame = lax.axis_index("ctx")

    def put(ahead, behind):
        for i, (own, out) in enumerate(((dk, key_out), (dv, value_out))):
            total = own[...] + jnp.where(frame < 15, ahead[i].astype(F32), 0.0)
            total += jnp.where(frame > 0, behind[i].astype(F32), 0.0)
            out[...] = total.astype(BF16)

    @pl.when(step < 2)
    def _():
        put(ahead0, behind0)

    @pl.when(step >= 2)
    def _():
        put(ahead1, behind1)


def any_spec():
    return pl.BlockSpec(memory_space=pl.ANY)


def vmem_spec():
    return pl.BlockSpec(memory_space=pltpu.VMEM)


def along_x(value, step):
    pairs = []
    for dp in range(8):
        for ctx in range(16):
            x = (ctx // 8) * 2 + dp % 2
            tx = (x + step) % 4
            pairs.append((dp * 16 + ctx, ((dp // 2) * 2 + tx % 2) * 16 + (tx // 2) * 8 + ctx % 8))
    return lax.ppermute(value, ("dp", "ctx"), pairs)


def along_z(value, step):
    return lax.ppermute(value, "dp", [(i, (i + 2 * step) % 8) for i in range(8)])


def shards(
    queries, key_rows, values, saved_out, log_sum, out_grad, out_weight, tile_coords, extents
):
    q, k, v, so, og = (a[0] for a in (queries, key_rows, values, saved_out, out_grad))
    pair = jax.ShapeDtypeStruct((2, TOK, HD), BF16)
    dma = pltpu.SemaphoreType.DMA
    moving = jax.ShapeDtypeStruct((2, 4, BLK, SUM_CUT), BF16)
    before, after, d_attn, keep_a, send_a, keep_b, send_b = pl.pallas_call(
        gather_kernel,
        out_shape=(pair, pair, jax.ShapeDtypeStruct((TOK, HD), BF16)) + (moving,) * 4,
        in_specs=[vmem_spec()] + [any_spec()] * 4,
        out_specs=(any_spec(),) * 7,
        scratch_shapes=[
            pltpu.VMEM((2, PAD, HALF), BF16),
            pltpu.VMEM((8, PAD, HALF), BF16),
            pltpu.VMEM((2, 16, BLK, HALF), BF16),
            pltpu.VMEM((TOK, HD), BF16),
            pltpu.VMEM((TOK, D), BF16),
            pltpu.VMEM((TOK, HD), BF16),
            pltpu.VMEM((TOK, HALF), BF16),
            pltpu.VMEM((4, BLK, SUM_CUT), BF16),
            pltpu.VMEM((TOK, HD), BF16),
        ] + [pltpu.VMEM((2, 4, BLK, SUM_CUT), BF16)] * 4 + [
            dma((7,)), dma((8,)), dma((2, 3)), dma((2, 4, 2)), dma((2, 4, 2)), dma((2, 16)),
            dma((2, 16)), dma((2, 16)), dma((2, 16)), dma((2,)), dma((2,)), dma((2,)), dma((8,)),
        ] + HALO_SEMS,
        compiler_params=pltpu.CompilerParams(
            collective_id=0, has_side_effects=True, vmem_limit_bytes=VMEM_LIMIT),
        cost_estimate=pl.CostEstimate(
            flops=10**10, bytes_accessed=20 * 10**6, transcendentals=0),
        name="gather",
    )(out_weight, k, v, so, og)
    got_a, got_b = along_z(send_a, 2), along_x(send_b, 2)

    own32 = jax.ShapeDtypeStruct((TOK, HD), F32)
    own16 = jax.ShapeDtypeStruct((TOK, HD), BF16)
    half_pair = jax.ShapeDtypeStruct((2, TOK, HD // 2), BF16)
    grads, towards = (), []
    for first in (0, H // 2):
        skip, wide = first // GROUP, GROUP * HEAD
        col = pl.BlockSpec((TOK, wide), lambda h, *_, skip=skip: (0, skip + h))
        row = pl.BlockSpec((GROUP, 1, TOK), lambda h, *_, skip=skip: (skip + h, 0, 0))
        sides = pl.BlockSpec((2, TOK, wide), lambda h, *_: (0, 0, h))
        k_side = pl.BlockSpec((None, TOK, wide), lambda h, *_, skip=skip: (0, 0, skip + h))
        v_side = pl.BlockSpec((None, TOK, wide), lambda h, *_, skip=skip: (1, 0, skip + h))
        *grads, to_prev, to_next = pl.pallas_call(
            functools.partial(attention_kernel, first),
            out_shape=(own16, own32, own32, half_pair, half_pair),
            grid_spec=pltpu.PrefetchScalarGridSpec(
                num_scalar_prefetch=2,
                grid=(H // 2 // GROUP,),
                in_specs=[col] * 3 + [k_side, v_side] * 2 + [col] * 2 + [row]
                + [any_spec()] * len(grads),
                out_specs=(col,) * 3 + (sides,) * 2,
                scratch_shapes=[
                    pltpu.SMEM((2, 3, 4), jnp.int32),
                    pltpu.VMEM((8, TOK), F32),
                    pltpu.VMEM((HEAD, TOK), F32),
                ],
            ),
            input_output_aliases={12 + i: i for i in range(len(grads))},
            compiler_params=pltpu.CompilerParams(vmem_limit_bytes=VMEM_LIMIT),
            cost_estimate=pl.CostEstimate(
                flops=6 * 10**9, bytes_accessed=15 * 10**6, transcendentals=5 * 10**6),
            name="attention",
        )(tile_coords, extents, q, k, v, before, before, after, after, d_attn, so,
          log_sum[0][:, None, :], *grads)
        towards.append((to_prev, to_next))
    dq, dk, dv = grads
    ahead = lax.ppermute(towards[0][0], "ctx", [(i + 1, i) for i in range(15)])
    behind = lax.ppermute(towards[0][1], "ctx", [(i, i + 1) for i in range(15)])

    weight_grad, from_next, from_prev = pl.pallas_call(
        scatter_kernel,
        out_shape=(jax.ShapeDtypeStruct((ROWS, D), F32), half_pair, half_pair),
        in_specs=[any_spec()] * 6,
        out_specs=(vmem_spec(), any_spec(), any_spec()),
        scratch_shapes=[pltpu.VMEM((2, 4, BLK, SUM_CUT), BF16)] * 4
        + [pltpu.VMEM((4, BLK, SUM_CUT), BF16)] * 6
        + [pltpu.VMEM((3, BLK, SUM_CUT), BF16)] * 2 + [
            pltpu.VMEM((8, PAD, HALF), BF16),
            pltpu.VMEM((8, PAD, HALF), BF16),
            dma((2, 2)), dma((2, 2)), dma((2, 3)), dma((2, 3)), dma((7,)), dma((8,)),
            dma((4,)),
        ] + HALO_SEMS,
        compiler_params=pltpu.CompilerParams(
            collective_id=1, has_side_effects=True, vmem_limit_bytes=VMEM_LIMIT),
        cost_estimate=pl.CostEstimate(
            flops=10**10, bytes_accessed=20 * 10**6, transcendentals=0),
        name="scatter",
    )(*towards[1], keep_a, got_a, keep_b, got_b)

    wide = HD // 4
    whole = pl.BlockSpec((TOK, wide), lambda i: (0, i))
    lower = pl.BlockSpec((2, TOK, wide), lambda i: (0, 0, jnp.minimum(i, 1)))
    upper = pl.BlockSpec((2, TOK, wide), lambda i: (0, 0, jnp.maximum(i - 2, 0)))
    key_grad, value_grad = pl.pallas_call(
        combine_kernel,
        out_shape=(own16, own16),
        grid=(4,),
        in_specs=[whole, whole, lower, lower, upper, upper],
        out_specs=(whole, whole),
        compiler_params=pltpu.CompilerParams(vmem_limit_bytes=VMEM_LIMIT),
        name="combine",
    )(dk, dv, ahead, behind, from_next, from_prev)
    return dq[None], key_grad[None], value_grad[None], weight_grad


def solution(mesh):
    return jax.shard_map(
        shards,
        mesh=mesh,
        in_specs=(
            P("dp", "ctx", None),
            P("dp", "ctx", None),
            P("dp", "ctx", None),
            P("dp", "ctx", None),
            P("dp", None, "ctx"),
            P("dp", "ctx", None),
            P(("dp", "ctx"), None),
            P(),
            P(),
        ),
        out_specs=(
            P("dp", "ctx", None),
            P("dp", "ctx", None),
            P("dp", "ctx", None),
            P(("dp", "ctx"), None),
        ),
        check_vma=False,
    )
```

```python
import functools
import functools
import math

import jax
import jax.numpy as jnp
from jax import lax
from jax.experimental import pallas as pl
from jax.experimental.pallas import tpu as pltpu
from jax.sharding import PartitionSpec as P

H = 12
HEAD = 128
TILE = 128
TOK = 512
HD = 1536
D = 3072
HALF = D // 2
ROWS = 12
PAD = 16
BLK = 8 * ROWS
CUT = 1024
PARTS = ((0, CUT), (CUT, HALF))
SUM_CUT = 768
SUM_PARTS = ((0, SUM_CUT), (SUM_CUT, HALF))
SUB = SUM_CUT // 2
STEPS = (1, 3, 2)
GROUP = 2
VMEM_LIMIT = 60 * 2**20
MESH = pl.DeviceIdType.MESH
F32 = jnp.float32
BF16 = jnp.bfloat16
LOG2E = math.log2(math.e)
NT = (((1,), (1,)), ((), ()))
TN = (((0,), (0,)), ((), ()))


def place():
    dp, ctx = lax.axis_index("dp"), lax.axis_index("ctx")
    return dp // 2, (ctx // 8) * 2 + dp % 2, (ctx // 2) % 4, ctx % 2


def device(z, x, y, c):
    return (z * 2 + x % 2, (x // 2) * 8 + y * 2 + c)


def block_of(z, x):
    return z * 4 + (x % 2) * 2 + x // 2


def remote(src, dst, send, recv, target):
    return pltpu.make_async_remote_copy(
        src_ref=src, dst_ref=dst, send_sem=send, recv_sem=recv,
        device_id=target, device_id_type=MESH,
    )


def greet(z, x, y, c):
    barrier = pltpu.get_barrier_semaphore()

    def tell(target):
        pl.semaphore_signal(barrier, inc=1, device_id=target, device_id_type=MESH)

    for dy in range(4):
        for dc in range(2):
            if dy or dc:
                tell(device(z, x, (y + dy) % 4, (c + dc) % 2))
    for step in STEPS:
        tell(device(z, (x + step) % 4, y, c))
        tell(device((z + step) % 4, x, y, c))

    ctx, dp = lax.axis_index("ctx"), lax.axis_index("dp")

    @pl.when(ctx == 7)
    def _():
        tell((dp, ctx + 1))

    @pl.when(ctx == 8)
    def _():
        tell((dp, ctx - 1))

    pl.semaphore_wait(barrier, 13 + jnp.where((ctx == 7) | (ctx == 8), 1, 0))


HALO_SEMS = [pltpu.SemaphoreType.DMA(shape) for shape in ((2,), (2,), (2, 4), (2, 4), (2, 4))]


class Halo:
    def __init__(self, ups, downs, before, after, send, recv, piece_send, piece_recv, relay_send):
        self.dp, self.ctx = lax.axis_index("dp"), lax.axis_index("ctx")
        ctx = self.ctx
        ways = (
            (ups, before, jnp.minimum(ctx + 1, 15), jnp.where(ctx == 7, 0, jnp.minimum(ctx + 1, 15)), 8),
            (downs, after, jnp.maximum(ctx - 1, 0), jnp.where(ctx == 8, 15, jnp.maximum(ctx - 1, 0)), 7),
        )
        self.straight, self.pieces, self.relays = [], [], []
        for i, (src, dst, near, first, last) in enumerate(ways):
            self.straight.append(
                remote(src[0], dst.at[0], send.at[i], recv.at[i], (self.dp, near)))
            spans = [pl.ds(j * TILE, TILE) for j in range(TOK // TILE)]
            self.pieces.append([
                remote(src[1].at[span], dst.at[1, span], piece_send.at[i, j], piece_recv.at[i, j],
                       (self.dp, first)) for j, span in enumerate(spans)])
            self.relays.append([
                remote(dst.at[1, span], dst.at[1, span], relay_send.at[i, j], piece_recv.at[i, j],
                       (self.dp, last)) for j, span in enumerate(spans)])
        self.sends = (ctx < 15, ctx > 0)
        self.gets = (ctx > 0, ctx < 15)
        self.passes = (ctx == 0, ctx == 15)
        self.far = (ctx == 7, ctx == 8)

    def start(self):
        for i in range(2):
            @pl.when(self.sends[i])
            def _():
                for copy in self.pieces[i]:
                    copy.start()

            @pl.when(self.sends[i] & jnp.logical_not(self.far[i]))
            def _():
                self.straight[i].start()

    def start_far(self):
        for i in range(2):
            @pl.when(self.far[i])
            def _():
                self.straight[i].start()

    def relay(self, *numbers):
        for i in range(2):
            @pl.when(self.passes[i])
            def _():
                for j in numbers:
                    self.pieces[i][j].wait_recv()
                    self.relays[i][j].start()

    def wait(self):
        for i in range(2):
            @pl.when(self.gets[i])
            def _():
                self.straight[i].wait_recv()
                for copy in self.pieces[i]:
                    copy.wait_recv()

            @pl.when(self.sends[i])
            def _():
                self.straight[i].wait_send()
                for copy in self.pieces[i]:
                    copy.wait_send()

            @pl.when(self.passes[i])
            def _():
                for onward in self.relays[i]:
                    onward.wait_send()


def gather_kernel(
    strip, keys, vals, so_hbm, og_hbm,
    before, after, d_attn_out, keep_a_out, send_a_out, keep_b_out, send_b_out,
    padded, strips, full, so, og, so_sib, og_sib, turn, d_attn, partial, keep_a, send_a, keep_b, send_b,
    strip_send, strip_recv, near_send, far_send, pass_send, ag_recv, late_recv, sib_send, sib_recv,
    ex_send, ex_recv, load_sem, store_sem, *halo_sems,
):
    z, x, y, c = place()
    sib = device(z, x, y, 1 - c)
    me = block_of(z, x)
    slot = y * 2 + c
    loads = [pltpu.make_async_copy(so_hbm, so, load_sem.at[0]),
             pltpu.make_async_copy(og_hbm, og, load_sem.at[1])]
    for copy in loads:
        copy.start()
    for h in range(2):
        padded[h, 0:ROWS] = strip[:, h * HALF:(h + 1) * HALF]
        padded[h, ROWS:PAD] = jnp.zeros((PAD - ROWS, HALF), BF16)
    strips[slot] = padded[c]
    greet(z, x, y, c)

    pending = []
    number = 0
    for dy in range(4):
        for dc in range(2):
            if dy or dc:
                tc = (c + dc) % 2
                copy = remote(padded.at[tc], strips.at[slot], strip_send.at[number],
                              strip_recv.at[slot], device(z, x, (y + dy) % 4, tc))
                copy.start()
                pending.append(copy)
                number += 1
    other = pl.ds(pl.multiple_of((1 - c) * HALF, HALF), HALF)
    exchange = [
        remote(so_hbm, so_sib, ex_send.at[0], ex_recv.at[0], sib),
        remote(og_hbm.at[:, other], og_sib, ex_send.at[1], ex_recv.at[1], sib),
    ]
    for copy in exchange:
        copy.start()
    for dy in range(4):
        for dc in range(2):
            if dy or dc:
                src = ((y + dy) % 4) * 2 + (c + dc) % 2
                remote(strips.at[src], strips.at[src], strip_send.at[0], strip_recv.at[src],
                       sib).wait_recv()
    row = lax.broadcasted_iota(jnp.int32, (BLK, 8 * PAD), 0)
    col = lax.broadcasted_iota(jnp.int32, (BLK, 8 * PAD), 1)
    pick = jnp.where(col == (row // ROWS) * PAD + row % ROWS, 1.0, 0.0).astype(BF16)
    for o in range(0, HALF, 768):
        full[c, me, :, o:o + 768] = jnp.dot(
            pick, strips[:, :, o:o + 768].reshape(8 * PAD, 768),
            preferred_element_type=F32).astype(BF16)

    def piece(half, block, part):
        low, high = PARTS[part]
        return full.at[half, block, :, low:high]

    def along(part, first, step):
        over_x = (part == 0) == first
        return device(z, (x + step) % 4, y, c) if over_x else device((z + step) % 4, x, y, c)

    def block_at(part, first, step):
        if part == 0:
            return block_of(z, (x + step) % 4)
        return block_of((z + step) % 4, x)

    for part in range(2):
        for i, step in enumerate(STEPS):
            copy = remote(piece(c, me, part), piece(c, me, part), near_send.at[part, i],
                          ag_recv.at[part, me], along(part, True, step))
            copy.start()
            pending.append(copy)

    def onward(part, block, j):
        for i, step in enumerate((1, 3)):
            copy = remote(piece(c, block, part), piece(c, block, part), far_send.at[part, j, i],
                          ag_recv.at[part, block], along(part, False, step))
            copy.start()
            pending.append(copy)

    def half_piece(block, part, upper):
        low, high = PARTS[part]
        return full.at[c, block, (BLK // 2 if upper else 0):(BLK if upper else BLK // 2), low:high]

    def pass_on(part, block, j, step):
        upper = step == 1
        copy = remote(half_piece(block, part, upper), half_piece(block, part, upper),
                      pass_send.at[part, j, int(upper)],
                      (late_recv if upper else ag_recv).at[part, block],
                      along(part, False, 4 - step))
        copy.start()
        pending.append(copy)

    def arrived_late(part, block):
        for upper, sem in ((False, ag_recv), (True, late_recv)):
            remote(half_piece(block, part, upper), half_piece(block, part, upper),
                   near_send.at[part, 0], sem.at[part, block], sib).wait_recv()

    def to_sibling(part, block):
        copy = remote(piece(c, block, part), piece(c, block, part), sib_send.at[part, block],
                      sib_recv.at[part, block], sib)
        copy.start()
        pending.append(copy)

    def arrived(part, block):
        remote(piece(c, block, part), piece(c, block, part), near_send.at[part, 0],
               ag_recv.at[part, block], sib).wait_recv()

    for part in range(2):
        onward(part, me, 0)
        to_sibling(part, me)

    halo = Halo((keys, vals), (keys, vals), before, after, *halo_sems)
    halo.start()
    for copy in exchange:
        copy.wait_recv()
    for copy in loads:
        copy.wait()
    def wgrad_group(group, j):
        rows = pl.ds(pl.multiple_of(group * 4 * BLK, 4 * BLK), 4 * BLK)
        for low, high in SUM_PARTS:
            cols = pl.ds(pl.multiple_of(c * HALF + low, 128), high - low)
            total = lax.dot_general(so[:, rows], og[:, cols], TN, preferred_element_type=F32)
            total += lax.dot_general(so_sib[:, rows], og_sib[:, low:high], TN,
                                     preferred_element_type=F32)
            total = total.astype(BF16).reshape(4, BLK, high - low)
            if low:
                turn[...] = total
            elif j == 0:
                keep_a[0] = total
            elif j == 2:
                send_a[0] = total
            else:
                first, other = (keep_a, send_a) if j == 1 else (send_a, keep_a)
                first[1, :, :, :SUB] = total[:, :, :SUB]
                other[1, :, :, SUB:] = total[:, :, SUB:]
        for k in range(4):
            tx = (x + k) % 4
            total = turn[(tx % 2) * 2 + tx // 2]
            if k == 0:
                keep_b[0, group] = total
            elif k == 2:
                send_b[0, group] = total
            else:
                first, other = (keep_b, send_b) if k == 1 else (send_b, keep_b)
                first[1, group, :, :SUB] = total[:, :SUB]
                other[1, group, :, SUB:] = total[:, SUB:]

    wgrad_group(z, 0)
    for j, step in enumerate(STEPS):
        for part in range(2):
            block = block_at(part, True, step)
            arrived(part, block)
            onward(part, block, j + 1)
            to_sibling(part, block)
        wgrad_group((z + j + 1) % 4, j + 1)
    halo.start_far()
    halo.relay(0)
    stores = []
    for j, (src, dst) in enumerate(((keep_a, keep_a_out), (send_a, send_a_out),
                                    (keep_b, keep_b_out), (send_b, send_b_out))):
        stores.append(pltpu.make_async_copy(src, dst, store_sem.at[j]))
        stores[-1].start()

    def far_block(part, step, inner):
        if part == 0:
            return block_of((z + step) % 4, (x + inner) % 4)
        return block_of((z + inner) % 4, (x + step) % 4)

    for j, inner in enumerate((0,) + STEPS):
        for step in (1, 3):
            for part in range(2):
                block = far_block(part, step, inner)
                arrived(part, block)
                pass_on(part, block, j, step)
                to_sibling(part, block)
        if j:
            halo.relay(j)
    def from_sibling(part, group):
        for inner in range(4):
            block = group * 4 + inner
            remote(piece(1 - c, block, part), piece(1 - c, block, part),
                   sib_send.at[part, block], sib_recv.at[part, block], sib).wait_recv()

    def project(part, group):
        low, high = PARTS[part]
        feats = pl.ds(pl.multiple_of(group * 4 * BLK, 4 * BLK), 4 * BLK)

        def some_rows(i, carry):
            rows = pl.ds(pl.multiple_of(i * 256, 256), 256)
            total = jnp.zeros((256, 4 * BLK), F32) if part == 0 else partial[rows, feats]
            for h in range(2):
                weight = full[h, pl.ds(group * 4, 4), :, low:high].reshape(4 * BLK, high - low)
                total += lax.dot_general(og[rows, h * HALF + low:h * HALF + high], weight, NT,
                                         preferred_element_type=F32)
            if part == 0:
                partial[rows, feats] = total
            else:
                d_attn[rows, feats] = total.astype(BF16)
            return carry

        from_sibling(part, group)
        lax.fori_loop(0, TOK // 256, some_rows, 0)

    for i, inner in enumerate((0,) + STEPS):
        if i < 3:
            project(0, (z + (0, 1, 3)[i]) % 4)
        for part in range(2):
            block = far_block(part, 2, inner)
            arrived_late(part, block)
            to_sibling(part, block)
    project(0, (z + 2) % 4)
    for step in (0,) + STEPS:
        group = (z + step) % 4
        project(1, group)
        feats = pl.ds(pl.multiple_of(group * 4 * BLK, 4 * BLK), 4 * BLK)
        stores.append(pltpu.make_async_copy(d_attn.at[:, feats], d_attn_out.at[:, feats],
                                            store_sem.at[4 + step]))
        stores[-1].start()
    halo.wait()
    for copy in stores:
        copy.wait()
    for copy in exchange:
        copy.wait_send()
    for copy in pending:
        copy.wait_send()


def scatter_kernel(
    to_prev, to_next, keep_a_in, got_a_in, keep_b_in, got_b_in,
    out, from_next, from_prev,
    keep_a, got_a, keep_b, got_b, pass_a, pass_b, more_a, more_b,
    sum_a, sum_b, got_a2, got_b2, packed, last,
    first_send, first_recv, second_send, second_recv, last_send, last_recv,
    load_sem, *halo_sems,
):
    z, x, y, c = place()
    slot = y * 2 + c
    (low_a, high_a), (low_b, high_b) = SUM_PARTS
    loads = []
    for j, (src, dst) in enumerate(((keep_a_in, keep_a), (got_a_in, got_a),
                                    (keep_b_in, keep_b), (got_b_in, got_b))):
        loads.append(pltpu.make_async_copy(src, dst, load_sem.at[j]))
        loads[-1].start()
    greet(z, x, y, c)
    halo = Halo((to_next.at[0], to_next.at[1]), (to_prev.at[0], to_prev.at[1]),
                from_prev, from_next, *halo_sems)
    for copy in loads:
        copy.wait()
    first = []
    for part, (keep, got, ready, more) in enumerate(
            ((keep_a, got_a, pass_a, more_a), (keep_b, got_b, pass_b, more_b))):
        for j in range(4):
            ready[j] = (keep[1, j].astype(F32) + got[1, j].astype(F32)).astype(BF16)
        for i, (cols, step) in enumerate(((slice(0, SUB), 1), (slice(SUB, 2 * SUB), 3))):
            target = device(z, (x + step) % 4, y, c) if part else device((z + step) % 4, x, y, c)
            copy = remote(ready.at[:, :, cols], more.at[:, :, cols], first_send.at[part, i],
                          first_recv.at[part, i], target)
            copy.start()
            first.append(copy)
    halo.start()
    for copy in first:
        copy.wait_recv()
    for keep, got, more, total_ref in (
            (keep_a, got_a, more_a, sum_a), (keep_b, got_b, more_b, sum_b)):
        for j in range(4):
            total = keep[0, j].astype(F32) + got[0, j].astype(F32) + more[j].astype(F32)
            total_ref[j] = total.astype(BF16)
    xs = (x % 2) * 2 + x // 2
    second = []
    for i, step in enumerate(STEPS):
        tz, tx = (z + step) % 4, (x + step) % 4
        for part, src, dst, target in (
            (0, sum_a.at[(tx % 2) * 2 + tx // 2], got_a2.at[i], device(z, tx, y, c)),
            (1, sum_b.at[tz], got_b2.at[i], device(tz, x, y, c)),
        ):
            copy = remote(src, dst, second_send.at[part, i], second_recv.at[part, i], target)
            copy.start()
            second.append(copy)
    halo.start_far()
    halo.relay(0, 1)
    for copy in second:
        copy.wait_recv()
    row = lax.broadcasted_iota(jnp.int32, (8 * PAD, BLK), 0)
    col = lax.broadcasted_iota(jnp.int32, (8 * PAD, BLK), 1)
    spread = jnp.where(
        (col == (row // PAD) * ROWS + row % PAD) & (row % PAD < ROWS), 1.0, 0.0).astype(BF16)
    total_a = sum_a[xs].astype(F32)
    total_b = sum_b[z].astype(F32)
    for i in range(3):
        total_a += got_a2[i].astype(F32)
        total_b += got_b2[i].astype(F32)
    packed[:, :, low_a:high_a] = jnp.dot(spread, total_a.astype(BF16), preferred_element_type=F32).astype(
        BF16).reshape(8, PAD, high_a - low_a)
    packed[:, :, low_b:high_b] = jnp.dot(spread, total_b.astype(BF16), preferred_element_type=F32).astype(
        BF16).reshape(8, PAD, high_b - low_b)
    number = 0
    third = []
    for dy in range(4):
        for dc in range(2):
            if dy or dc:
                ty, tc = (y + dy) % 4, (c + dc) % 2
                copy = remote(packed.at[ty * 2 + tc], last.at[slot], last_send.at[number],
                              last_recv.at[slot], device(z, x, ty, tc))
                copy.start()
                third.append(copy)
                number += 1
    halo.relay(2, 3)
    last[slot] = packed[slot]
    for dy in range(4):
        for dc in range(2):
            if dy or dc:
                src = ((y + dy) % 4) * 2 + (c + dc) % 2
                remote(packed.at[src], last.at[src], last_send.at[0], last_recv.at[src],
                       device(z, x, y, 1 - c)).wait_recv()
    for h in range(2):
        total = last[h].astype(F32)
        for i in range(1, 4):
            total += last[2 * i + h].astype(F32)
        out[:, h * HALF:(h + 1) * HALF] = total[:ROWS] * (1.0 / 256.0)
    halo.wait()
    for copy in first + second + third:
        copy.wait_send()


def attention_kernel(
    first, coords, extents,
    q_all, k_all, v_all, kp_all, vp_all, kn_all, vn_all, a_all, o_all, lse_all, *refs,
):
    outputs, (table, row_s, dqt_s) = refs[-8:-3], refs[-3:]
    begin = first + pl.program_id(0) * GROUP
    frame = lax.axis_index("ctx")

    @pl.when(begin == first)
    def _():
        for k in range(3):
            base = jnp.clip(frame + k - 1, 0, 15) * 4
            for t in range(4):
                r, col = coords[base + t, 1], coords[base + t, 2]
                table[0, k, r * 2 + col] = t
                table[1, k, col * 2 + r] = t

    def one_head(j, carry):
        cols = pl.ds(pl.multiple_of(j * HEAD, HEAD), HEAD)
        flat = [ref.at[:, cols] for ref in (
            q_all, k_all, v_all, kp_all, vp_all, kn_all, vn_all, a_all, o_all) + outputs[:3]]
        sides = [ref.at[:, :, cols] for ref in outputs[3:]]
        head_kernel(begin + j, frame, extents, *flat[:9], lse_all.at[j], *flat[9:], *sides,
                    table, row_s, dqt_s)
        return carry

    lax.fori_loop(0, GROUP, one_head, 0)


def head_kernel(
    head, frame, extents,
    q_ref, k_ref, v_ref, kp_ref, vp_ref, kn_ref, vn_ref, a_ref, o_ref, lse_ref,
    dq_ref, dk_ref, dv_ref, prev_ref, next_ref, table, row_s, dqt_s,
):
    scale = HEAD ** (-0.5)
    near_f, near_r, near_c = extents[head, 0], extents[head, 1], extents[head, 2]
    order = jnp.where(near_c == 0, 1, 0)
    keys, vals = (kp_ref, k_ref, kn_ref), (vp_ref, v_ref, vn_ref)
    outs = ((prev_ref.at[0], prev_ref.at[1]), (dk_ref, dv_ref), (next_ref.at[0], next_ref.at[1]))

    def spot(k, s):
        return pl.ds(pl.multiple_of(table[order, k, s] * TILE, TILE), TILE)

    def rows_of(ref, k, begin, size, whole):
        if whole:
            return ref[begin:begin + size, :]
        tiles = [ref[spot(k, s), :] for s in range(begin // TILE, (begin + size) // TILE)]
        return tiles[0] if len(tiles) == 1 else jnp.concatenate(tiles, axis=0)

    def line_of(i, begin, size, whole):
        if whole:
            return row_s[i:i + 1, begin:begin + size]
        tiles = [row_s[i:i + 1, spot(1, s)] for s in range(begin // TILE, (begin + size) // TILE)]
        return tiles[0] if len(tiles) == 1 else jnp.concatenate(tiles, axis=1)

    def frame_of(k, size):
        whole = size == TOK
        step = min(size, 256)
        queries = [
            (rows_of(q_ref, 1, at, size, whole), rows_of(a_ref, 1, at, size, whole),
             line_of(0, at, size, whole), line_of(1, at, size, whole))
            for at in range(0, TOK, size)]
        units = [(g, at) for g in range(TOK // size) for at in range(g * size, (g + 1) * size, step)]
        ready = []
        for g, at in units:
            q, a, lse, delta = queries[g]
            key = rows_of(keys[k], k, at, step, whole)
            scores = lax.dot_general(key, q, NT, preferred_element_type=F32)
            d_probs = lax.dot_general(rows_of(vals[k], k, at, step, whole), a, NT,
                                      preferred_element_type=F32)
            ready.append((key, scores, d_probs))
        halves = []
        for (g, at), (key, scores, d_probs) in zip(units, ready):
            q, a, lse, delta = queries[g]
            probs = jnp.exp2(scores * (scale * LOG2E) - lse)
            halves.append((probs.astype(BF16), (probs * (d_probs - delta)).astype(BF16)))
        sums = [None] * (TOK // size)
        for (g, at), (key, _, _), (probs, d_scores) in zip(units, ready, halves):
            q, a, lse, delta = queries[g]
            dv = jnp.dot(probs, a, preferred_element_type=F32)
            dk = jnp.dot(d_scores, q, preferred_element_type=F32) * scale
            dqt = jnp.dot(key.T, d_scores, preferred_element_type=F32)
            sums[g] = dqt if sums[g] is None else sums[g] + dqt
            for ref, value in zip(outs[k], (dk, dv)):
                if whole:
                    ref[at:at + step, :] = value.astype(ref.dtype)
                else:
                    for i in range(step // TILE):
                        ref[spot(k, at // TILE + i), :] = value[i * TILE:(i + 1) * TILE].astype(
                            ref.dtype)
        for g, total in enumerate(sums):
            span = slice(g * size, (g + 1) * size)
            if k == 1:
                dqt_s[:, span] = total
            else:
                dqt_s[:, span] += total

    wide = near_r * near_c == 1
    modes = ((TOK, wide), (256, near_r + near_c == 1), (TILE, near_r + near_c == 0))
    ones = jnp.ones((8, HEAD), BF16)
    prod = a_ref[...].astype(F32) * o_ref[...].astype(F32)
    high = prod.astype(BF16)
    low = (prod - high.astype(F32)).astype(BF16)
    delta = lax.dot_general(ones, high, NT, preferred_element_type=F32)
    delta += lax.dot_general(ones, low, NT, preferred_element_type=F32)
    row_s[0:1, :] = lse_ref[...] * LOG2E
    row_s[1:2, :] = delta[0:1]
    for size, here in modes:
        @pl.when(here)
        def _():
            frame_of(1, size)

    for k, there, ref in ((0, frame > 0, prev_ref), (2, frame < 15, next_ref)):
        use = (near_f == 1) & there
        for size, here in modes:
            @pl.when(use & here)
            def _():
                frame_of(k, size)

        @pl.when(jnp.logical_not(use))
        def _():
            ref[...] = jnp.zeros_like(ref)

    @pl.when(wide)
    def _():
        dq_ref[...] = (dqt_s[...].T * scale).astype(BF16)

    @pl.when(jnp.logical_not(wide))
    def _():
        for s in range(4):
            dq_ref[spot(1, s), :] = (dqt_s[:, s * TILE:(s + 1) * TILE].T * scale).astype(BF16)


def combine_kernel(dk, dv, ahead0, behind0, ahead1, behind1, key_out, value_out):
    step = pl.program_id(0)
    frame = lax.axis_index("ctx")

    def put(ahead, behind):
        for i, (own, out) in enumerate(((dk, key_out), (dv, value_out))):
            total = own[...] + jnp.where(frame < 15, ahead[i].astype(F32), 0.0)
            total += jnp.where(frame > 0, behind[i].astype(F32), 0.0)
            out[...] = total.astype(BF16)

    @pl.when(step < 2)
    def _():
        put(ahead0, behind0)

    @pl.when(step >= 2)
    def _():
        put(ahead1, behind1)


def any_spec():
    return pl.BlockSpec(memory_space=pl.ANY)


def vmem_spec():
    return pl.BlockSpec(memory_space=pltpu.VMEM)


def along_x(value, step):
    pairs = []
    for dp in range(8):
        for ctx in range(16):
            x = (ctx // 8) * 2 + dp % 2
            tx = (x + step) % 4
            pairs.append((dp * 16 + ctx, ((dp // 2) * 2 + tx % 2) * 16 + (tx // 2) * 8 + ctx % 8))
    return lax.ppermute(value, ("dp", "ctx"), pairs)


def along_z(value, step):
    return lax.ppermute(value, "dp", [(i, (i + 2 * step) % 8) for i in range(8)])


def shards(
    queries, key_rows, values, saved_out, log_sum, out_grad, out_weight, tile_coords, extents
):
    q, k, v, so, og = (a[0] for a in (queries, key_rows, values, saved_out, out_grad))
    pair = jax.ShapeDtypeStruct((2, TOK, HD), BF16)
    dma = pltpu.SemaphoreType.DMA
    moving = jax.ShapeDtypeStruct((2, 4, BLK, SUM_CUT), BF16)
    before, after, d_attn, keep_a, send_a, keep_b, send_b = pl.pallas_call(
        gather_kernel,
        out_shape=(pair, pair, jax.ShapeDtypeStruct((TOK, HD), BF16)) + (moving,) * 4,
        in_specs=[vmem_spec()] + [any_spec()] * 4,
        out_specs=(any_spec(),) * 7,
        scratch_shapes=[
            pltpu.VMEM((2, PAD, HALF), BF16),
            pltpu.VMEM((8, PAD, HALF), BF16),
            pltpu.VMEM((2, 16, BLK, HALF), BF16),
            pltpu.VMEM((TOK, HD), BF16),
            pltpu.VMEM((TOK, D), BF16),
            pltpu.VMEM((TOK, HD), BF16),
            pltpu.VMEM((TOK, HALF), BF16),
            pltpu.VMEM((4, BLK, SUM_CUT), BF16),
            pltpu.VMEM((TOK, HD), BF16),
            pltpu.VMEM((TOK, HD), F32),
        ] + [pltpu.VMEM((2, 4, BLK, SUM_CUT), BF16)] * 4 + [
            dma((7,)), dma((8,)), dma((2, 3)), dma((2, 4, 2)), dma((2, 4, 2)), dma((2, 16)),
            dma((2, 16)), dma((2, 16)), dma((2, 16)), dma((2,)), dma((2,)), dma((2,)), dma((8,)),
        ] + HALO_SEMS,
        compiler_params=pltpu.CompilerParams(
            collective_id=0, has_side_effects=True, vmem_limit_bytes=VMEM_LIMIT),
        cost_estimate=pl.CostEstimate(
            flops=10**10, bytes_accessed=20 * 10**6, transcendentals=0),
        name="gather",
    )(out_weight, k, v, so, og)
    got_a, got_b = along_z(send_a, 2), along_x(send_b, 2)

    own32 = jax.ShapeDtypeStruct((TOK, HD), F32)
    own16 = jax.ShapeDtypeStruct((TOK, HD), BF16)
    half_pair = jax.ShapeDtypeStruct((2, TOK, HD // 2), BF16)
    grads, towards = (), []
    for first in (0, H // 2):
        skip, wide = first // GROUP, GROUP * HEAD
        col = pl.BlockSpec((TOK, wide), lambda h, *_, skip=skip: (0, skip + h))
        row = pl.BlockSpec((GROUP, 1, TOK), lambda h, *_, skip=skip: (skip + h, 0, 0))
        sides = pl.BlockSpec((2, TOK, wide), lambda h, *_: (0, 0, h))
        k_side = pl.BlockSpec((None, TOK, wide), lambda h, *_, skip=skip: (0, 0, skip + h))
        v_side = pl.BlockSpec((None, TOK, wide), lambda h, *_, skip=skip: (1, 0, skip + h))
        *grads, to_prev, to_next = pl.pallas_call(
            functools.partial(attention_kernel, first),
            out_shape=(own16, own32, own32, half_pair, half_pair),
            grid_spec=pltpu.PrefetchScalarGridSpec(
                num_scalar_prefetch=2,
                grid=(H // 2 // GROUP,),
                in_specs=[col] * 3 + [k_side, v_side] * 2 + [col] * 2 + [row]
                + [any_spec()] * len(grads),
                out_specs=(col,) * 3 + (sides,) * 2,
                scratch_shapes=[
                    pltpu.SMEM((2, 3, 4), jnp.int32),
                    pltpu.VMEM((8, TOK), F32),
                    pltpu.VMEM((HEAD, TOK), F32),
                ],
            ),
            input_output_aliases={12 + i: i for i in range(len(grads))},
            compiler_params=pltpu.CompilerParams(vmem_limit_bytes=VMEM_LIMIT),
            cost_estimate=pl.CostEstimate(
                flops=6 * 10**9, bytes_accessed=15 * 10**6, transcendentals=5 * 10**6),
            name="attention",
        )(tile_coords, extents, q, k, v, before, before, after, after, d_attn, so,
          log_sum[0][:, None, :], *grads)
        towards.append((to_prev, to_next))
    dq, dk, dv = grads
    ahead = lax.ppermute(towards[0][0], "ctx", [(i + 1, i) for i in range(15)])
    behind = lax.ppermute(towards[0][1], "ctx", [(i, i + 1) for i in range(15)])

    weight_grad, from_next, from_prev = pl.pallas_call(
        scatter_kernel,
        out_shape=(jax.ShapeDtypeStruct((ROWS, D), F32), half_pair, half_pair),
        in_specs=[any_spec()] * 6,
        out_specs=(vmem_spec(), any_spec(), any_spec()),
        scratch_shapes=[pltpu.VMEM((2, 4, BLK, SUM_CUT), BF16)] * 4
        + [pltpu.VMEM((4, BLK, SUM_CUT), BF16)] * 6
        + [pltpu.VMEM((3, BLK, SUM_CUT), BF16)] * 2 + [
            pltpu.VMEM((8, PAD, HALF), BF16),
            pltpu.VMEM((8, PAD, HALF), BF16),
            dma((2, 2)), dma((2, 2)), dma((2, 3)), dma((2, 3)), dma((7,)), dma((8,)),
            dma((4,)),
        ] + HALO_SEMS,
        compiler_params=pltpu.CompilerParams(
            collective_id=1, has_side_effects=True, vmem_limit_bytes=VMEM_LIMIT),
        cost_estimate=pl.CostEstimate(
            flops=10**10, bytes_accessed=20 * 10**6, transcendentals=0),
        name="scatter",
    )(*towards[1], keep_a, got_a, keep_b, got_b)

    wide = HD // 4
    whole = pl.BlockSpec((TOK, wide), lambda i: (0, i))
    lower = pl.BlockSpec((2, TOK, wide), lambda i: (0, 0, jnp.minimum(i, 1)))
    upper = pl.BlockSpec((2, TOK, wide), lambda i: (0, 0, jnp.maximum(i - 2, 0)))
    key_grad, value_grad = pl.pallas_call(
        combine_kernel,
        out_shape=(own16, own16),
        grid=(4,),
        in_specs=[whole, whole, lower, lower, upper, upper],
        out_specs=(whole, whole),
        compiler_params=pltpu.CompilerParams(vmem_limit_bytes=VMEM_LIMIT),
        name="combine",
    )(dk, dv, ahead, behind, from_next, from_prev)
    return dq[None], key_grad[None], value_grad[None], weight_grad


def solution(mesh):
    return jax.shard_map(
        shards,
        mesh=mesh,
        in_specs=(
            P("dp", "ctx", None),
            P("dp", "ctx", None),
            P("dp", "ctx", None),
            P("dp", "ctx", None),
            P("dp", None, "ctx"),
            P("dp", "ctx", None),
            P(("dp", "ctx"), None),
            P(),
            P(),
        ),
        out_specs=(
            P("dp", "ctx", None),
            P("dp", "ctx", None),
            P("dp", "ctx", None),
            P(("dp", "ctx"), None),
        ),
        check_vma=False,
    )
```
